256 devices in a mesh: samp: 16 (over z, core), var: 16 (over x, y).
Axes of the slice: x: 4, y: 4, z: 8, core: 2. Of those that a mesh axis runs over, the one named last changes fastest.
Arguments:
- geno: bfloat16 [8192, 32768], P('samp', 'var'), may hold values from 0 to 2
- covar: bfloat16 [8192, 32], P('samp')
- pheno: float32 [8192, 64], P('samp', 'var')
- perm: int32 [48, 8192], P(None, 'samp'), may hold values from 0 to 8191, each once within a row
- windows: int32 [64, 2], replicated, may hold values from 0 to 32768, as said below
Outputs:
- curves: float32 [64, 64], P('var')
- peak: float32 [64, 48], P('var')
The draws below stay inside these ranges and needn't reach their ends.
Inputs may be any that keep to these rules, and one draw needn't show every extreme that they name: Each gene g has windows[g, 0] < windows[g, 1], and its window lies within variants g // 4 * 2048 - 1024 to (g // 4 + 1) * 2048 + 1024, cut to the genome; in each band the first gene's window begins and the last gene's window ends at those bounds (cut to the genome).
All inputs are finite; a program needn't handle non-finite values.
Results may differ from the reference program's by a relative error of at most 0.0016.
Values may be sent and summed in bfloat16 or wider, within the bound.
A program may use at most 64 MiB of HBM per device.

```python
import jax
import jax.numpy as jnp
from jax import lax

VBAND = 2048
GENES_BAND = 4
PERMS = 48
COVS = 32
LEVELS = 64
NSAMP = 8192
GENES = 64
NVAR_TOTAL = 32768
REACH = 1024
N_VAR = 16


def covariate_base(key):
    return jax.random.normal(jax.random.fold_in(key, 11), (NSAMP, COVS), jnp.float32)


def draw_covar(key, part):
    return covariate_base(key).astype(jnp.bfloat16)


def draw_pheno(key, part):
    base = covariate_base(key)
    gene = jnp.arange(GENES, dtype=jnp.int32)
    first = base[:, gene % COVS]
    second = base[:, (gene * 7 + 3) % COVS]
    noise = jax.random.normal(jax.random.fold_in(key, 12), (NSAMP, GENES), jnp.float32)
    return noise + 2.0 * first + second


def draw_windows(key, part):
    gene = jnp.arange(GENES, dtype=jnp.int32)
    band = gene // GENES_BAND
    slot = gene % GENES_BAND
    centre = band * VBAND + jax.random.randint(jax.random.fold_in(key, 21), (GENES,), 0, VBAND)
    half = jax.random.randint(jax.random.fold_in(key, 22), (GENES,), REACH // 2, REACH + 1)
    start = centre - half
    end = centre + half + 1
    start = jnp.where(slot == 0, band * VBAND - REACH, start)
    end = jnp.where(slot == GENES_BAND - 1, (band + 1) * VBAND + REACH, end)
    start = jnp.clip(start, 0, NVAR_TOTAL - 1)
    end = jnp.clip(end, 1, NVAR_TOTAL)
    return jnp.stack([start, end], axis=1).astype(jnp.int32)


def block_scale(own_key, dims, split, smallest, largest):
    factor_of, own = 1.0, jax.random.fold_in(own_key, 6)
    for dim, blocks in split:
        steps = jnp.exp(jax.random.uniform(jax.random.fold_in(own, dim), (blocks,), jnp.float32, smallest / len(split), largest / len(split)))
        factor_of = factor_of * jnp.repeat(steps, dims[dim] // blocks).reshape([-1 if axis == dim else 1 for axis in range(len(dims))])
    return factor_of


def setup_inputs(seed: int = 0) -> dict:
    key_of = jax.random.split(jax.random.key(seed), 6)
    geno = jnp.clip(2.0 * jax.random.uniform(key_of[0], (NSAMP, NVAR_TOTAL), jnp.float32) ** block_scale(key_of[0], (NSAMP, NVAR_TOTAL), ((0, 16), (1, 16)), -0.2, 0.2), 0.0, 2.0).astype(jnp.bfloat16)
    covar = draw_covar(jax.random.fold_in(key_of[5], 71), 0)
    pheno = draw_pheno(jax.random.fold_in(key_of[5], 71), 0)
    perm = jax.vmap(lambda own: jax.random.permutation(own, NSAMP))(jax.random.split(key_of[3], PERMS)).reshape((PERMS, NSAMP)).astype(jnp.int32)
    windows = draw_windows(jax.random.fold_in(key_of[5], 71), 0)
    return dict(geno=geno, covar=covar, pheno=pheno, perm=perm, windows=windows)


EPS = 1e-06
LEVMAX = 40.0

def factor_solve(factor, rhs):
    lower_part = lax.linalg.triangular_solve(factor, rhs, left_side=True, lower=True)
    return lax.linalg.triangular_solve(factor, lower_part, left_side=True, lower=True, transpose_a=True)

def reference(geno, covar, pheno, perm, windows):
    nsamp = geno.shape[0]
    ones = jnp.ones((nsamp, 1), jnp.bfloat16)
    xlow = jnp.concatenate([ones, covar], axis=1)
    xmat = xlow.astype(jnp.float32)
    cross = jnp.dot(xmat.T, xmat, precision=lax.Precision.HIGHEST)
    factor = jnp.linalg.cholesky(cross)
    beta_y = factor_solve(factor, jnp.dot(xmat.T, pheno, precision=lax.Precision.HIGHEST))
    gcross = jnp.dot(xlow.T.astype(jnp.float32), geno.astype(jnp.float32), preferred_element_type=jnp.float32)
    beta_g = factor_solve(factor, gcross)
    yres = pheno - jnp.dot(xmat, beta_y, precision=lax.Precision.HIGHEST)
    ynorm = jnp.sqrt(lax.optimization_barrier(jnp.sum(yres * yres, axis=0)) + EPS)
    shuffled = jnp.take(yres, perm, axis=0)
    scaled = (shuffled / ynorm[None, None, :]).astype(jnp.bfloat16)
    ycols = jnp.transpose(scaled, (1, 2, 0)).reshape(nsamp, GENES * PERMS)
    width = 2 * VBAND

    def per_band(band):
        start = jnp.clip(band * VBAND - REACH, 0, NVAR_TOTAL - width).astype(jnp.int32)
        block = lax.dynamic_slice_in_dim(geno, start, width, 1).astype(jnp.float32)
        coef = lax.dynamic_slice_in_dim(beta_g, start, width, 1)
        gres = block - jnp.dot(xmat, coef, precision=lax.Precision.HIGHEST)
        gsq = lax.optimization_barrier(jnp.sum(gres * gres, axis=0))
        cols = lax.dynamic_slice_in_dim(ycols, (band * GENES_BAND * PERMS).astype(jnp.int32), GENES_BAND * PERMS, 1).astype(jnp.float32)
        numer = jnp.dot(gres.T, cols, precision=lax.Precision.HIGHEST)
        corr = numer / jnp.sqrt(gsq + EPS)[:, None]
        squared = (corr * corr).reshape(width, GENES_BAND, PERMS)
        window = lax.dynamic_slice_in_dim(windows, (band * GENES_BAND).astype(jnp.int32), GENES_BAND, 0)
        position = start + jnp.arange(width, dtype=jnp.int32)
        inside = (position[:, None] >= window[None, :, 0]) & (position[:, None] < window[None, :, 1])
        return lax.optimization_barrier(jnp.max(jnp.where(inside[:, :, None], squared, 0.0), axis=0))
    peak_sq = lax.map(per_band, jnp.arange(N_VAR, dtype=jnp.int32)).reshape(GENES, PERMS)
    peak = jnp.float32(nsamp) * peak_sq
    levels = LEVMAX * jnp.arange(LEVELS, dtype=jnp.float32) / (LEVELS - 1)
    curves = lax.optimization_barrier(jnp.mean(jax.nn.sigmoid(peak[:, :, None] - levels[None, None, :]), axis=1))
    return (curves, peak)
```

```python
import functools

import jax
import jax.numpy as jnp
from jax import lax
from jax.experimental import pallas as pl
from jax.experimental.pallas import tpu as pltpu
from jax.sharding import PartitionSpec as P

MESH = pl.DeviceIdType.MESH
F32 = jnp.float32
BF16 = jnp.bfloat16
HIGH = lax.Precision.HIGHEST

EPS = 1e-06
LEVMAX = 40.0
LEVELS = 64

NZ = 8
NB = 16
NS = 512
NSAMP = 8192
VB = 2048
VH = 1024
NG = 4
NP = 48
NC = 32
XR = 48
ONE = 44
SPARE = 45
ROWS = NG * NP
CH = ROWS // NZ
DW = VH + 128
HOPS = (4, 3)


def nt(a, b):
    return lax.dot_general(a, b, (((1,), (1,)), ((), ())), preferred_element_type=F32)


def mm(a, b, precision=None):
    return lax.dot_general(
        a, b, (((1,), (0,)), ((), ())), preferred_element_type=F32, precision=precision
    )


def kernel(
    upto,
    geno, covt, phet, perm, win,
    cur_ref, peak_ref,
    xa, p8, gs, gcp, gr, ga, gm, yt, yo, yn, ds, rb, xs, xm, fm,
    loc_sem, xg_s, xg_r, ring_s, ring_r, fw_s, fw_r, gr_s, gr_r, ga_s, ga_r,
    y_s, y_r, rs_s, rs_r, x_s, x_r, f_s, f_r,
):
    s = lax.axis_index("samp")
    b = lax.axis_index("var")
    z = lax.div(s, 2)
    c = lax.rem(s, 2)
    oc = 1 - c
    up_band = lax.rem(b + 1, NB)
    down_band = lax.rem(b + NB - 1, NB)
    nbr = lax.rem(b + 2 * c - 1 + NB, NB)

    def zc(k):
        return lax.rem(z + (k + NZ), NZ)

    def dev(zz, cc, bb):
        return {"samp": zz * 2 + cc, "var": bb}

    def copy(src, dst, ss, rs, to):
        return pltpu.make_async_remote_copy(
            src_ref=src, dst_ref=dst, send_sem=ss, recv_sem=rs,
            device_id=to, device_id_type=MESH,
        )

    pend = []

    def start(src, dst, ss, rs, to):
        d = copy(src, dst, ss, rs, to)
        d.start()
        pend.append(d)

    def landed(dst, rs):
        copy(dst, dst, rs, rs, dev(z, oc, b)).wait_recv()

    def finish():
        for d in pend:
            d.wait_send()

    def stop():
        finish()
        cur_ref[...] = jnp.zeros_like(cur_ref)
        peak_ref[...] = jnp.zeros_like(peak_ref)

    own_geno = pltpu.make_async_copy(
        geno.at[:, pl.ds(pl.multiple_of(c * VH, VH), VH)], gs.at[c], loc_sem
    )
    own_geno.start()
    p8[0:4, :] = phet[...]
    p8[4:8, :] = phet[...]
    full = p8[...]
    hi = full.astype(BF16).astype(F32)
    rest = full - hi
    mid = rest.astype(BF16).astype(F32)
    low = (rest - mid).astype(BF16).astype(F32)
    row8 = lax.broadcasted_iota(jnp.int32, (8, NS), 0)
    block_a = jnp.where(row8 < 4, hi, mid)
    block_b = jnp.where(row8 < 4, low, jnp.where(row8 == 4, 1.0, 0.0))
    xa[s] = jnp.concatenate([covt[...].astype(F32), block_a, block_b], axis=0).astype(BF16)

    barrier = pltpu.get_barrier_semaphore()
    peers = [dev(zc(k), c, b) for k in range(1, NZ)] + [dev(z, oc, b)]
    peers += [dev(z, cc, bb) for cc in (0, 1) for bb in (up_band, down_band)]
    for peer in peers:
        pl.semaphore_signal(barrier, inc=1, device_id=peer, device_id_type=MESH)
    pl.semaphore_wait(barrier, len(peers))

    start(
        geno.at[:, pl.ds(pl.multiple_of(oc * VH, VH), VH)], gs.at[c], xg_s, xg_r, dev(z, oc, b)
    )

    def slot(k, cc):
        return zc(k) * 2 + cc

    def send_right(t):
        q = slot(-t, c)
        start(xa.at[q], xa.at[q], ring_s.at[0, t], ring_r.at[0, t], dev(zc(1), c, b))

    def send_left(t):
        q = slot(t, c)
        start(xa.at[q], xa.at[q], ring_s.at[1, t], ring_r.at[1, t], dev(zc(-1), c, b))

    def hand_over(k):
        q = slot(k, c)
        start(xa.at[q], xa.at[q], fw_s.at[k + 4], fw_r.at[k + 4], dev(z, oc, b))

    def got_right(t):
        landed(xa.at[slot(-1 - t, c)], ring_r.at[0, t])

    def got_left(t):
        landed(xa.at[slot(1 + t, c)], ring_r.at[1, t])

    send_right(0)
    send_left(0)
    hand_over(0)
    got_right(0)
    send_right(1)
    hand_over(-1)
    got_left(0)
    send_left(1)
    hand_over(1)

    own_geno.wait()
    landed(gs.at[oc], xg_r)
    landed(xa.at[slot(0, oc)], fw_r.at[4])
    gpart = mm(xa[z * 2], gs[0]) + mm(xa[z * 2 + 1], gs[1])

    got_right(1)
    send_right(2)
    hand_over(-2)
    got_left(1)
    send_left(2)
    hand_over(2)

    mean = gpart[ONE:ONE + 1, :] * (1.0 / (2 * NS))

    def spread(i, acc):
        blk = gs[lax.div(i, 32), pl.ds(pl.multiple_of(lax.rem(i, 32) * 16, 16), 16), :].astype(F32)
        dif = blk - mean
        return acc + dif * dif

    acc = lax.fori_loop(0, 64, spread, jnp.zeros((16, VH), F32))
    local_sq = jnp.sum(acc, axis=0, keepdims=True)
    rowg = lax.broadcasted_iota(jnp.int32, (XR, VH), 0)
    gpart = jnp.where(rowg == SPARE, local_sq, gpart)
    for j in range(NZ):
        gcp[j] = gpart[:, j * 128:(j + 1) * 128]
    for k in range(1, NZ):
        start(gcp.at[zc(k)], gr.at[z], gr_s.at[k], gr_r.at[NZ - k], dev(zc(k), c, b))

    got_right(2)
    send_right(3)
    hand_over(-3)
    got_left(2)
    hand_over(3)
    got_right(3)
    hand_over(-4)
    for k in (-1, 1, -2, 2, -3, 3, -4):
        landed(xa.at[slot(k, oc)], fw_r.at[k + 4])
    if upto == 1:
        for k in range(1, NZ):
            landed(gr.at[zc(k)], gr_r.at[k])
        stop()
        return

    def gram_step(i, acc):
        blk = xa[i]
        return acc + nt(blk, blk)

    gram = lax.fori_loop(0, 2 * NZ, gram_step, jnp.zeros((XR, XR), F32))
    gm[...] = jnp.zeros_like(gm)
    gm[:, 0:XR] = gram
    a = gm[...]
    colmean = a[:, ONE:ONE + 1] * (1.0 / NSAMP)
    row = lax.broadcasted_iota(jnp.int32, (XR, 128), 0)
    lane = lax.broadcasted_iota(jnp.int32, (XR, 128), 1)
    for k in (ONE,) + tuple(range(NC)):
        q = a[:, k:k + 1]
        r = a[k:k + 1, :]
        inv = 1.0 / a[k:k + 1, k:k + 1]
        rr = r * inv
        nxt = a - q * rr
        nxt = jnp.where(row == k, rr, nxt)
        nxt = jnp.where(lane == k, jnp.where(row == k, -inv, q * inv), nxt)
        a = nxt
    in_row = (row < NC) | (row == ONE)
    in_lane = (lane < NC) | (lane == ONE)
    gm[...] = jnp.where(in_row & in_lane, -a, 0.0)

    for k in range(1, NZ):
        landed(gr.at[zc(k)], gr_r.at[k])
    gr[z] = gcp[z]
    tot = gr[0]
    for j in range(1, NZ):
        tot = tot + gr[j]
    mu = tot[ONE:ONE + 1, :] * (1.0 / NSAMP)
    between = jnp.zeros((1, 128), F32)
    for j in range(NZ):
        off = gr[j, ONE:ONE + 1, :] * (1.0 / (2 * NS)) - mu
        between = between + off * off
    ga[z] = tot + jnp.where(row == SPARE, between * (2.0 * NS), 0.0)
    for k in range(1, NZ):
        start(ga.at[z], ga.at[z], ga_s.at[k], ga_r.at[NZ - k], dev(zc(k), c, b))

    ba = a[32:40, :]
    beta = ba + pltpu.roll(ba, 4, axis=0) + a[40:48, :]
    r8 = lax.broadcasted_iota(jnp.int32, (8, 128), 0)
    l8 = lax.broadcasted_iota(jnp.int32, (8, 128), 1)
    pick = (l8 == r8 + 32) | (l8 == r8 + 36) | (l8 == r8 + 40)
    coef = jnp.where(pick & (r8 < 4), 1.0, 0.0)
    coef = jnp.where(((l8 < NC) | (l8 == ONE)) & (r8 < 4), -beta, coef)
    c_hi = coef.astype(BF16).astype(F32)
    c_rest = coef - c_hi
    c_mid = c_rest.astype(BF16).astype(F32)
    c_low = c_rest - c_mid
    coefs = jnp.concatenate([c_hi, c_mid, c_low], axis=0)[:, 0:XR].astype(BF16)

    def resid(i, acc):
        t = mm(coefs, xa[i])
        y = (t[16:24] + t[8:16]) + t[0:8]
        yt[i] = y
        return acc + y * y

    ysq = jnp.sum(
        lax.fori_loop(0, 2 * NZ, resid, jnp.zeros((8, NS), F32)), axis=1, keepdims=True
    )
    ynorm = jnp.sqrt(ysq + EPS)

    def scale(i, carry):
        yt[i] = (yt[i] / ynorm).astype(BF16).astype(F32)
        return carry

    lax.fori_loop(0, 2 * NZ, scale, 0)
    if upto == 2:
        for k in range(1, NZ):
            landed(ga.at[zc(k)], ga_r.at[k])
        stop()
        return

    for blk in range(NS // 128):
        idx = perm[:, blk * 128:(blk + 1) * 128]
        ilo = lax.bitwise_and(idx, 127)
        ihi = lax.shift_right_logical(idx, 7)

        def look(i, accs, ilo=ilo, ihi=ihi):
            accs = list(accs)
            for q in range(4):
                hit = ihi == i * 4 + q
                for g in range(NG):
                    src = jnp.broadcast_to(yt[i, g:g + 1, q * 128:(q + 1) * 128], (NP, 128))
                    got = jnp.take_along_axis(src, ilo, axis=1, mode="promise_in_bounds")
                    accs[g] = jnp.where(hit, got, accs[g])
            return tuple(accs)

        accs = lax.fori_loop(
            0, 2 * NZ, look, tuple(jnp.zeros((NP, 128), F32) for _ in range(NG))
        )
        for g in range(NG):
            yo[c, g * NP:(g + 1) * NP, blk * 128:(blk + 1) * 128] = accs[g].astype(BF16)
    if upto == 3:
        for k in range(1, NZ):
            landed(ga.at[zc(k)], ga_r.at[k])
        stop()
        return

    start(yo.at[c], yo.at[c], y_s.at[0], y_r.at[0], dev(z, oc, b))
    start(yo.at[c], yn.at[c], y_s.at[1], y_r.at[1 + c], dev(z, 0, up_band))
    start(yo.at[c], yn.at[c], y_s.at[2], y_r.at[1 + c], dev(z, 1, down_band))

    def product(y, kind):
        ds[kind, :, 0:VH] = mm(y[0], gs[0]) + mm(y[1], gs[1])
        ds[kind, :, VH:DW] = jnp.zeros((ROWS, 128), F32)
        ds[kind, :, VH:VH + XR] = nt(y[0], xa[z * 2]) + nt(y[1], xa[z * 2 + 1])

    def chunk(kind, k):
        return ds.at[kind, pl.ds(pl.multiple_of(zc(k) * CH, CH), CH)]

    def hops(kind, way):
        return HOPS[(kind + way) % 2]

    def send_sum(kind, way, t):
        n = hops(kind, way)
        sign = 1 - 2 * way
        mine = chunk(kind, -sign * (n - t))
        if t == 0:
            src = mine
        else:
            src = rb.at[kind, way, t - 1]
            landed(src, rs_r.at[kind, way, t - 1])
            src[...] = src[...] + mine[...]
        start(
            src, rb.at[kind, way, t], rs_s.at[kind, way, t], rs_r.at[kind, way, t],
            dev(zc(-sign), c, b),
        )

    landed(yo.at[oc], y_r.at[0])
    product(yo, 0)
    send_sum(0, 0, 0)
    send_sum(0, 1, 0)
    landed(yn.at[0], y_r.at[1])
    landed(yn.at[1], y_r.at[2])
    product(yn, 1)
    send_sum(1, 1, 0)
    send_sum(1, 0, 0)

    for k in range(1, NZ):
        landed(ga.at[zc(k)], ga_r.at[k])
    if upto == 4:
        for kind in range(2):
            for way in range(2):
                landed(rb.at[kind, way, 0], rs_r.at[kind, way, 0])
        stop()
        return

    gx = jnp.concatenate([ga[j] for j in range(NZ)], axis=1)
    total_sq = gx[SPARE:SPARE + 1, :]
    ones_row = gx[ONE:ONE + 1, :]
    inv = gm[:, 0:XR]
    centred = jnp.where(rowg < NC, gx - colmean * ones_row, 0.0)
    explained = jnp.sum(centred * mm(inv, centred, HIGH), axis=0, keepdims=True)
    weight = 1.0 / (jnp.maximum(total_sq - explained, 0.0) + EPS)
    beta_g = mm(inv, jnp.where((rowg < NC) | (rowg == ONE), gx, 0.0), HIGH)

    for t in range(1, 4):
        for kind, way in ((0, 0), (0, 1), (1, 1), (1, 0)):
            if t < hops(kind, way):
                send_sum(kind, way, t)

    at = b * VB + c * VH + lax.broadcasted_iota(jnp.int32, (CH, VH), 1)
    gene = lax.div(z, 2)

    def largest(kind, owner):
        total = chunk(kind, 0)[...]
        for way in range(2):
            last = hops(kind, way) - 1
            landed(rb.at[kind, way, last], rs_r.at[kind, way, last])
            total = total + rb[kind, way, last]
        numer = total[:, 0:VH] - mm(total[:, VH:VH + XR], beta_g, HIGH)
        first = win[0, owner * NG + gene]
        last = win[1, owner * NG + gene]
        inside = (at >= first) & (at < last)
        best = jnp.max(jnp.where(inside, numer * numer * weight, 0.0), axis=1, keepdims=True)
        return jnp.broadcast_to(best, (CH, 128))

    xs[0] = largest(0, b)
    start(xs.at[0], xm.at[0], x_s.at[0], x_r.at[0], dev(z, oc, b))
    xs[1] = largest(1, nbr)
    start(xs.at[1], xm.at[2 - c], x_s.at[1], x_r.at[2 - c], dev(z, c, nbr))
    start(xs.at[1], xm.at[2 - c], x_s.at[2], x_r.at[2 - c], dev(z, oc, nbr))
    for j in range(3):
        landed(xm.at[j], x_r.at[j])
    best = jnp.maximum(jnp.maximum(xs[0], xm[0]), jnp.maximum(xm[1], xm[2])) * float(NSAMP)

    r24 = lax.broadcasted_iota(jnp.int32, (CH, 128), 0)
    l24 = lax.broadcasted_iota(jnp.int32, (CH, 128), 1)
    peaks = jnp.sum(
        jnp.where(l24 == r24 + CH * lax.rem(z, 2), best, 0.0), axis=0, keepdims=True
    )
    level = LEVMAX * l24.astype(F32) / (LEVELS - 1)
    curve = jnp.sum(jax.nn.sigmoid(best - level), axis=0, keepdims=True)
    r8 = lax.broadcasted_iota(jnp.int32, (8, 128), 0)
    fm[z] = jnp.where(r8 == 0, peaks, jnp.where(r8 == 1, curve, 0.0))
    for k in range(1, NZ):
        start(fm.at[z], fm.at[z], f_s.at[k], f_r.at[NZ - k], dev(zc(k), c, b))
    for k in range(1, NZ):
        landed(fm.at[zc(k)], f_r.at[k])
    for g in range(NG):
        both = fm[2 * g] + fm[2 * g + 1]
        peak_ref[g:g + 1, :] = both[0:1, 0:NP]
        cur_ref[g:g + 1, :] = both[1:2, 0:LEVELS] * (1.0 / NP)
    finish()


def per_device(upto, geno, covar, pheno, perm, windows):
    dma = pltpu.SemaphoreType.DMA
    vmem = pltpu.VMEM
    spec = pl.BlockSpec(memory_space=pltpu.VMEM)
    return pl.pallas_call(
        functools.partial(kernel, upto),
        out_shape=(
            jax.ShapeDtypeStruct((NG, LEVELS), F32),
            jax.ShapeDtypeStruct((NG, NP), F32),
        ),
        in_specs=[
            pl.BlockSpec(memory_space=pl.ANY), spec, spec, spec,
            pl.BlockSpec(memory_space=pltpu.SMEM),
        ],
        out_specs=(spec, spec),
        scratch_shapes=[
            vmem((2 * NZ, XR, NS), BF16),
            vmem((8, NS), F32),
            vmem((2, NS, VH), BF16),
            vmem((NZ, XR, 128), F32),
            vmem((NZ, XR, 128), F32),
            vmem((NZ, XR, 128), F32),
            vmem((XR, 128), F32),
            vmem((2 * NZ, 8, NS), F32),
            vmem((2, ROWS, NS), BF16),
            vmem((2, ROWS, NS), BF16),
            vmem((2, ROWS, DW), F32),
            vmem((2, 2, 4, CH, DW), F32),
            vmem((2, CH, 128), F32),
            vmem((3, CH, 128), F32),
            vmem((NZ, 8, 128), F32),
            dma, dma, dma,
            dma((2, 4)), dma((2, 4)),
            dma((NZ,)), dma((NZ,)),
            dma((NZ,)), dma((NZ,)),
            dma((NZ,)), dma((NZ,)),
            dma((3,)), dma((3,)),
            dma((2, 2, 4)), dma((2, 2, 4)),
            dma((3,)), dma((3,)),
            dma((NZ,)), dma((NZ,)),
        ],
        compiler_params=pltpu.CompilerParams(
            collective_id=0, has_side_effects=True, vmem_limit_bytes=40 * 1024 * 1024
        ),
        name="scan",
    )(geno, covar.T, pheno.T, perm, windows.T)


def build(mesh, upto):
    in_specs = (P("samp", "var"), P("samp", None), P("samp", "var"), P(None, "samp"), P())
    out_specs = (P("var", None), P("var", None))
    return jax.shard_map(
        functools.partial(per_device, upto), mesh=mesh, in_specs=in_specs, out_specs=out_specs,
        check_vma=False,
    )


def solution(mesh):
    return build(mesh, 9)
```

```python
import functools

import jax
import jax.numpy as jnp
from jax import lax
from jax.experimental import pallas as pl
from jax.experimental.pallas import tpu as pltpu
from jax.sharding import PartitionSpec as P

MESH = pl.DeviceIdType.MESH
F32 = jnp.float32
BF16 = jnp.bfloat16
HIGH = lax.Precision.HIGHEST

EPS = 1e-06
LEVMAX = 40.0
LEVELS = 64

NZ = 8
NB = 16
NS = 512
NSAMP = 8192
VB = 2048
VH = 1024
NG = 4
NP = 48
NC = 32
XR = 48
ONE = 44
SPARE = 45
GR = 40
GONE = 36
GSP = 37
ROWS = NG * NP
CH = ROWS // NZ
DW = VH + 128
HOPS = (4, 3)
LO = 256
TR = NSAMP // LO * NG
PZ = NP // NZ


def nt(a, b):
    return lax.dot_general(a, b, (((1,), (1,)), ((), ())), preferred_element_type=F32)


def mm(a, b, precision=None):
    return lax.dot_general(
        a, b, (((1,), (0,)), ((), ())), preferred_element_type=F32, precision=precision
    )


def iota(shape, dim):
    return lax.broadcasted_iota(jnp.int32, shape, dim)


def fold_rows(v):
    head, body, tail = v[0:32], v[32:40], v[40:48]
    low = iota(body.shape, 0) < 4
    return jnp.concatenate(
        [head, jnp.where(low, body + pltpu.roll(body, 4, axis=0) + tail, tail)], axis=0
    )


def kernel(
    upto,
    geno, covh, pheh, permh, winh,
    cur_ref, peak_ref,
    perm, win, xc, xy, xp, gs, gg, pk, gm, gcp, gr, ga, gh, yt, tab, yo, ds, rb, xs, xm, fm,
    in_sem, geno_sem, g1_s, g1_r, p_s, p_r, pk_s, pk_r, c_s, c_r, f_s, f_r, h_s, h_r,
    gr_s, gr_r, ga_s, ga_r, gh_s, gh_r, t_s, t_r, y_s, y_r, rs_s, rs_r, x_s, x_r, o_s, o_r,
):
    s = lax.axis_index("samp")
    b = lax.axis_index("var")
    z = lax.div(s, 2)
    c = lax.rem(s, 2)
    oc = 1 - c
    up_band = lax.rem(b + 1, NB)
    down_band = lax.rem(b + NB - 1, NB)
    nbr = lax.rem(b + 2 * c - 1 + NB, NB)
    own_at = pl.multiple_of(oc * VH, VH)
    halo_at = pl.multiple_of(c * VH, VH)

    def zc(k):
        return lax.rem(z + (k + NZ), NZ)

    def dev(zz, cc, bb):
        return {"samp": zz * 2 + cc, "var": bb}

    def half(cc):
        return pl.ds(pl.multiple_of(cc * VH, VH), VH)

    sent, due = [], {}

    def start(key, src, dst, ss, rs, to, here, here_sem):
        d = pltpu.make_async_remote_copy(
            src_ref=src, dst_ref=dst, send_sem=ss, recv_sem=rs, device_id=to, device_id_type=MESH
        )
        d.start()
        sent.append(d)
        due[key] = (here, here_sem)

    def landed(key):
        here, sem = due.pop(key)
        pltpu.make_async_remote_copy(
            src_ref=here, dst_ref=here, send_sem=sem, recv_sem=sem,
            device_id=dev(z, oc, b), device_id_type=MESH,
        ).wait_recv()

    def stop():
        for key in list(due):
            landed(key)
        for d in sent:
            d.wait_send()

    def cut(level):
        if upto != level:
            return False
        stop()
        cur_ref[...] = jnp.zeros_like(cur_ref)
        peak_ref[...] = jnp.zeros_like(peak_ref)
        return True

    other = dev(z, oc, b)
    loads = [
        pltpu.make_async_copy(src, dst, in_sem.at[i])
        for i, (src, dst) in enumerate((
            (covh, xc.at[z]), (pheh, xy.at[z]), (permh, perm), (winh, win),
        ))
    ]
    for d in loads:
        d.start()
    barrier = pltpu.get_barrier_semaphore()
    peers = [dev(zc(k), c, b) for k in range(1, NZ)] + [other]
    peers += [dev(z, cc, bb) for cc in (0, 1) for bb in (up_band, down_band)]
    for peer in peers:
        pl.semaphore_signal(barrier, inc=1, device_id=peer, device_id_type=MESH)
    own_geno = pltpu.make_async_copy(geno.at[:, half(c)], gs.at[c, :, pl.ds(own_at, VH)], geno_sem)
    own_geno.start()
    for d in loads:
        d.wait()

    phe = xy[z]
    full = jnp.concatenate([phe, phe], axis=0)
    hi = full.astype(BF16).astype(F32)
    rest = full - hi
    mid = rest.astype(BF16).astype(F32)
    low = (rest - mid).astype(BF16).astype(F32)
    row8 = iota((8, NS), 0)
    block_a = jnp.where(row8 < 4, hi, mid)
    block_b = jnp.where(row8 < 4, low, jnp.where(row8 == 4, 1.0, 0.0))
    xp[c] = jnp.concatenate([xc[z].astype(F32), block_a, block_b], axis=0).astype(BF16)
    mine = xp[c]
    gg[c] = jnp.zeros((GR, 128), F32)
    gg[c, :, 0:XR] = fold_rows(nt(mine, mine))

    pl.semaphore_wait(barrier, len(peers))
    start("g1", gg.at[c], gg.at[c], g1_s, g1_r, other, gg.at[oc], g1_r)
    start("p", xp.at[c], xp.at[c], p_s, p_r, other, xp.at[oc], p_r)
    if cut(0):
        own_geno.wait()
        return

    landed("g1")
    g = gg[0] + gg[1]
    lane40 = iota((GR, 128), 1)
    g = jnp.where(lane40 < GONE, g, pltpu.roll(g, 128 - (ONE - GONE), axis=1))
    g = jnp.concatenate([g, jnp.zeros((8, 128), F32)], axis=0)
    lane16 = iota((16, 128), 1)
    pk[z] = jnp.where(
        lane16 < GR, g[0:16],
        jnp.where(lane16 < 2 * GR, pltpu.roll(g[16:32], GR, axis=1),
                  jnp.where(lane16 < 3 * GR, pltpu.roll(g[32:48], 2 * GR, axis=1), 0.0)),
    )
    near = (1, 7, 2, 6, 3, 5, 4)
    for k in near:
        start(("pk", k), pk.at[z], pk.at[z], pk_s.at[k], pk_r.at[NZ - k], dev(zc(k), c, b),
              pk.at[zc(k)], pk_r.at[k])
    start("f", geno.at[:, half(oc)], gs.at[c, :, half(c)], f_s, f_r, other,
          gs.at[oc, :, pl.ds(own_at, VH)], f_r)
    for k in near:
        to = dev(zc(k), c, b)
        start(("c", k), xc.at[z], xc.at[z], c_s.at[0, k], c_r.at[0, NZ - k], to,
              xc.at[zc(k)], c_r.at[0, k])
        start(("y", k), xy.at[z], xy.at[z], c_s.at[1, k], c_r.at[1, NZ - k], to,
              xy.at[zc(k)], c_r.at[1, k])
    halo = gs.at[0, :, pl.ds(halo_at, VH)], gs.at[1, :, pl.ds(halo_at, VH)]
    start("h0", geno.at[:, VH:2 * VH], gs.at[c, :, 0:VH], h_s.at[0], h_r.at[c],
          dev(z, 0, up_band), halo[0], h_r.at[0])
    start("h1", geno.at[:, 0:VH], gs.at[c, :, VH:2 * VH], h_s.at[1], h_r.at[c],
          dev(z, 1, down_band), halo[1], h_r.at[1])

    own_geno.wait()
    landed("f")
    landed("p")
    gpart = fold_rows(
        mm(xp[0], gs[0, :, pl.ds(own_at, VH)]) + mm(xp[1], gs[1, :, pl.ds(own_at, VH)])
    )
    mean = gpart[GONE:GONE + 1, :] * (1.0 / (2 * NS))

    def spread(i, acc):
        at = pl.ds(pl.multiple_of(lax.rem(i, 32) * 16, 16), 16)
        dif = gs[lax.div(i, 32), at, pl.ds(own_at, VH)].astype(F32) - mean
        return acc + dif * dif

    acc = lax.fori_loop(0, 64, spread, jnp.zeros((16, VH), F32))
    rowg = iota((GR, VH), 0)
    gpart = jnp.where(rowg == GSP, jnp.sum(acc, axis=0, keepdims=True), gpart)
    for j in range(NZ):
        gcp[j] = gpart[:, j * 128:(j + 1) * 128]

    for k in range(1, NZ):
        landed(("pk", k))
    if cut(1):
        return
    tot = pk[0]
    for j in range(1, NZ):
        tot = tot + pk[j]
    a = jnp.concatenate(
        [tot, pltpu.roll(tot, 128 - GR, axis=1), pltpu.roll(tot, 128 - 2 * GR, axis=1)[0:8]], axis=0
    )
    row, lane = iota((GR, 128), 0), iota((GR, 128), 1)
    in_row = (row < NC) | (row == GONE)
    in_lane = (lane < NC) | (lane == GONE)
    a = jnp.where(in_lane, a, 0.0)
    colmean = a[:, GONE:GONE + 1] * (1.0 / NSAMP)
    for k in (GONE,) + tuple(range(NC)):
        q = a[:, k:k + 1]
        r = a[k:k + 1, :]
        inv = 1.0 / a[k:k + 1, k:k + 1]
        rr = r * inv
        nxt = a - q * rr
        nxt = jnp.where(row == k, rr, nxt)
        nxt = jnp.where(lane == k, jnp.where(row == k, -inv, q * inv), nxt)
        a = nxt
    gm[...] = jnp.where(in_row & in_lane, -a, 0.0)
    for k in near:
        start(("gr", k), gcp.at[zc(k)], gr.at[z], gr_s.at[k], gr_r.at[NZ - k], dev(zc(k), c, b),
              gr.at[zc(k)], gr_r.at[k])

    beta = a[32:40, :]
    row24 = beta.astype(BF16).astype(F32)
    rest = beta - row24
    mid = rest.astype(BF16).astype(F32)
    coefs = jnp.concatenate([row24, mid, rest - mid], axis=0)[:, 0:NC].astype(BF16)
    const = beta[0:4, GONE:GONE + 1]
    if cut(2):
        return
    for k in (0,) + near:
        if k:
            landed(("c", k))
            landed(("y", k))
        t = mm(coefs, xc[zc(k)])
        fit = (t[16:24] + t[8:16]) + t[0:8]
        yt[c, zc(k)] = xy[zc(k)] - (fit[0:4] + const)
    start("t", yt.at[c], yt.at[c], t_s, t_r, other, yt.at[oc], t_r)

    for k in range(1, NZ):
        landed(("gr", k))
    gr[z] = gcp[z]
    tot = gr[0]
    for j in range(1, NZ):
        tot = tot + gr[j]
    mu = tot[GONE:GONE + 1, :] * (1.0 / NSAMP)
    between = jnp.zeros((1, 128), F32)
    for j in range(NZ):
        off = gr[j, GONE:GONE + 1, :] * (1.0 / (2 * NS)) - mu
        between = between + off * off
    ga[z] = tot + jnp.where(row == GSP, between * (2.0 * NS), 0.0)
    for k in near:
        start(("ga", k), ga.at[z], ga.at[z], ga_s.at[k], ga_r.at[NZ - k], dev(zc(k), c, b),
              ga.at[zc(k)], ga_r.at[k])

    landed("t")
    ysq = jnp.zeros((NG, NS), F32)
    for cc in range(2):
        for j in range(NZ):
            ysq = ysq + yt[cc, j] * yt[cc, j]
    ynorm = jnp.sqrt(jnp.sum(ysq, axis=1, keepdims=True) + EPS)
    for cc in range(2):
        for j in range(NZ):
            y = yt[cc, j] / ynorm
            for q in range(2):
                at = (2 * (2 * j + cc) + q) * NG
                tab[at:at + NG, :] = y[:, q * LO:(q + 1) * LO]
    if cut(3):
        return

    table = tab[...].astype(BF16)
    count = iota((LO, NS), 0).astype(F32).astype(BF16)
    holds = lax.shift_right_logical(iota((TR, NS), 0), 2)
    low_half = iota((8, NS), 0) < NG
    one = jnp.ones((), BF16)
    zero = jnp.zeros((), BF16)

    def look(i, carry):
        got = []
        for u in range(4):
            idx = perm[pl.ds(i * 4 + u, 1), :]
            ilo = lax.bitwise_and(idx, LO - 1).astype(F32).astype(BF16)
            found = mm(table, jnp.where(count == ilo, one, zero))
            found = jnp.where(holds == lax.shift_right_logical(idx, 8), found, 0.0)
            part = found[0:8]
            for j in range(1, TR // 8):
                part = part + found[j * 8:(j + 1) * 8]
            got.append(part + pltpu.roll(part, NG, axis=0))
        rows = jnp.concatenate(
            [jnp.where(low_half, got[0], got[1]), jnp.where(low_half, got[2], got[3])], axis=0
        )
        yo[c, pl.ds(pl.multiple_of(i * 16, 16), 16), :] = rows.astype(BF16)
        return carry

    for j in range(3):
        lax.fori_loop(j * 4, j * 4 + 4, look, 0)
        part = pl.ds(j * 64, 64)
        start(("yo", j), yo.at[c, part], yo.at[c, part], y_s.at[j], y_r.at[j], other,
              yo.at[oc, part], y_r.at[j])
    if cut(4):
        return
    for j in range(3):
        landed(("yo", j))

    def product(kind, at):
        ds[kind, :, 0:VH] = mm(yo[0], gs[0, :, pl.ds(at, VH)]) + mm(yo[1], gs[1, :, pl.ds(at, VH)])

    def chunk(kind, k):
        return ds.at[kind, pl.ds(pl.multiple_of(zc(k) * CH, CH), CH)]

    def hops(kind, way):
        return HOPS[(kind + way) % 2]

    def send_sum(kind, way, t):
        n = hops(kind, way)
        sign = 1 - 2 * way
        mine = chunk(kind, -sign * (n - t))
        if t == 0:
            src = mine
        else:
            src = rb.at[kind, way, t - 1]
            landed(("rs", kind, way, t - 1))
            src[...] = src[...] + mine[...]
        start(
            ("rs", kind, way, t), src, rb.at[kind, way, t], rs_s.at[kind, way, t],
            rs_r.at[kind, way, t], dev(zc(-sign), c, b),
            rb.at[kind, way, t], rs_r.at[kind, way, t],
        )

    ds[0, :, VH:DW] = jnp.zeros((ROWS, 128), F32)
    ds[1, :, VH:DW] = jnp.zeros((ROWS, 128), F32)
    ds[0, :, VH:VH + XR] = nt(yo[0], xp[0]) + nt(yo[1], xp[1])
    product(0, own_at)
    send_sum(0, 0, 0)
    send_sum(0, 1, 0)
    landed("h0")
    landed("h1")
    product(1, halo_at)
    send_sum(1, 1, 0)
    send_sum(1, 0, 0)
    if cut(5):
        return

    for k in range(1, NZ):
        landed(("ga", k))
    start("gh", ga, gh, gh_s, gh_r, dev(z, oc, nbr), gh, gh_r)

    inv = gm[:, 0:GR]

    def of_variants(ref):
        gx = jnp.concatenate([ref[j] for j in range(NZ)], axis=1)
        centred = jnp.where(rowg < NC, gx - colmean * gx[GONE:GONE + 1, :], 0.0)
        explained = jnp.sum(centred * mm(inv, centred, HIGH), axis=0, keepdims=True)
        weight = 1.0 / (jnp.maximum(gx[GSP:GSP + 1, :] - explained, 0.0) + EPS)
        return mm(inv, jnp.where((rowg < NC) | (rowg == GONE), gx, 0.0), HIGH), weight

    beta_own, weight_own = of_variants(ga)
    order = ((0, 0), (0, 1), (1, 1), (1, 0))
    for kind, way in order:
        send_sum(kind, way, 1)
    landed("gh")
    beta_halo, weight_halo = of_variants(gh)
    for t in range(2, 4):
        for kind, way in order:
            if t < hops(kind, way):
                send_sum(kind, way, t)

    gene24 = lax.rem(iota((CH, 1), 0), NG)
    first = jnp.zeros((CH, 1), jnp.int32)
    last = jnp.zeros((CH, 1), jnp.int32)
    for g in range(NG):
        first = jnp.where(gene24 == g, win[0, b * NG + g], first)
        last = jnp.where(gene24 == g, win[1, b * NG + g], last)
    base = b * VB - VH + c * VB + iota((CH, VH), 1)

    sums = []
    for kind in range(2):
        total = chunk(kind, 0)[...]
        for way in range(2):
            end = hops(kind, way) - 1
            landed(("rs", kind, way, end))
            total = total + rb[kind, way, end]
        sums.append(total)
    if cut(6):
        return
    proj = jnp.where(iota((CH, XR), 1) < 32, sums[0][:, VH:VH + XR], 0.0)
    l48 = iota((CH, XR), 1)
    proj = jnp.where(l48 == GONE, sums[0][:, VH + ONE:VH + ONE + 1], proj)[:, 0:GR]

    def largest(kind, at, beta_g, weight):
        numer = sums[kind][:, 0:VH] - mm(proj, beta_g, HIGH)
        pos = base + at
        inside = (pos >= first) & (pos < last)
        return jnp.max(jnp.where(inside, numer * numer * weight, 0.0), axis=1, keepdims=True)

    best = jnp.maximum(
        largest(0, own_at, beta_own, weight_own), largest(1, halo_at, beta_halo, weight_halo)
    )
    xs[...] = jnp.broadcast_to(best, (CH, 128))
    start("x", xs, xm, x_s, x_r, other, xm, x_r)
    landed("x")
    best = jnp.maximum(xs[...], xm[...]) * float(NSAMP)

    r24, l24 = iota((CH, 128), 0), iota((CH, 128), 1)
    placed = jnp.where(l24 == lax.shift_right_logical(r24, 2) + PZ * z, best, 0.0)
    level = LEVMAX * l24.astype(F32) / (LEVELS - 1)
    curve = jax.nn.sigmoid(best - level)

    def over_perms(v):
        v = (v[0:8] + v[8:16]) + v[16:24]
        return v + pltpu.roll(v, NG, axis=0)

    fm[z] = jnp.where(iota((8, 128), 0) < NG, over_perms(placed), over_perms(curve))
    for k in near:
        start(("o", k), fm.at[z], fm.at[z], o_s.at[k], o_r.at[NZ - k], dev(zc(k), c, b),
              fm.at[zc(k)], o_r.at[k])
    for k in range(1, NZ):
        landed(("o", k))
    both = fm[0]
    for j in range(1, NZ):
        both = both + fm[j]
    peak_ref[...] = both[0:NG, 0:NP]
    cur_ref[...] = both[NG:2 * NG, 0:LEVELS] * (1.0 / NP)
    stop()


def per_device(upto, geno, covar, pheno, perm, windows):
    dma = pltpu.SemaphoreType.DMA
    vmem = pltpu.VMEM
    spec = pl.BlockSpec(memory_space=pltpu.VMEM)
    return pl.pallas_call(
        functools.partial(kernel, upto),
        out_shape=(
            jax.ShapeDtypeStruct((NG, LEVELS), F32),
            jax.ShapeDtypeStruct((NG, NP), F32),
        ),
        in_specs=[pl.BlockSpec(memory_space=pltpu.HBM)] * 5,
        out_specs=(spec, spec),
        scratch_shapes=[
            vmem((NP, NS), jnp.int32),
            pltpu.SMEM((2, NG * NB), jnp.int32),
            vmem((NZ, NC, NS), BF16),
            vmem((NZ, NG, NS), F32),
            vmem((2, XR, NS), BF16),
            vmem((2, NS, VB), BF16),
            vmem((2, GR, 128), F32),
            vmem((NZ, 16, 128), F32),
            vmem((GR, 128), F32),
            vmem((NZ, GR, 128), F32),
            vmem((NZ, GR, 128), F32),
            vmem((NZ, GR, 128), F32),
            vmem((NZ, GR, 128), F32),
            vmem((2, NZ, NG, NS), F32),
            vmem((TR, LO), F32),
            vmem((2, ROWS, NS), BF16),
            vmem((2, ROWS, DW), F32),
            vmem((2, 2, 4, CH, DW), F32),
            vmem((CH, 128), F32),
            vmem((CH, 128), F32),
            vmem((NZ, 8, 128), F32),
            dma((4,)), dma,
            dma, dma, dma, dma,
            dma((NZ,)), dma((NZ,)),
            dma((2, NZ)), dma((2, NZ)),
            dma, dma,
            dma((2,)), dma((2,)),
            dma((NZ,)), dma((NZ,)),
            dma((NZ,)), dma((NZ,)),
            dma, dma, dma, dma,
            dma((3,)), dma((3,)),
            dma((2, 2, 4)), dma((2, 2, 4)),
            dma, dma,
            dma((NZ,)), dma((NZ,)),
        ],
        compiler_params=pltpu.CompilerParams(
            collective_id=0, has_side_effects=True, vmem_limit_bytes=56 * 1024 * 1024
        ),
        name="scan",
    )(geno, covar.T, pheno.T, perm, windows.T)


def build(mesh, upto):
    in_specs = (P("samp", "var"), P("samp", None), P("samp", "var"), P(None, "samp"), P())
    out_specs = (P("var", None), P("var", None))
    return jax.shard_map(
        functools.partial(per_device, upto), mesh=mesh, in_specs=in_specs, out_specs=out_specs,
        check_vma=False,
    )


def solution(mesh):
    return build(mesh, 9)
```

```python
import functools

import jax
import jax.numpy as jnp
from jax import lax
from jax.experimental import pallas as pl
from jax.experimental.pallas import tpu as pltpu
from jax.sharding import PartitionSpec as P

MESH = pl.DeviceIdType.MESH
F32 = jnp.float32
BF16 = jnp.bfloat16
HIGH = lax.Precision.HIGHEST

EPS = 1e-06
LEVMAX = 40.0
LEVELS = 64

NZ = 8
NB = 16
NS = 512
NSAMP = 8192
VB = 2048
VH = 1024
NG = 4
NP = 48
NC = 32
XR = 48
ONE = 44
SPARE = 45
GR = 40
GONE = 36
GSP = 37
ROWS = NG * NP
CH = ROWS // NZ
HW = VH // 2
QMAX = 32767.0
TINY = 1e-30
HOPS = (4, 3)
LO = 256
TR = NSAMP // LO * NG
PZ = NP // NZ


def nt(a, b):
    return lax.dot_general(a, b, (((1,), (1,)), ((), ())), preferred_element_type=F32)


def mm(a, b, precision=None):
    return lax.dot_general(
        a, b, (((1,), (0,)), ((), ())), preferred_element_type=F32, precision=precision
    )


def iota(shape, dim):
    return lax.broadcasted_iota(jnp.int32, shape, dim)


def fold_rows(v):
    head, body, tail = v[0:32], v[32:40], v[40:48]
    low = iota(body.shape, 0) < 4
    return jnp.concatenate(
        [head, jnp.where(low, body + pltpu.roll(body, 4, axis=0) + tail, tail)], axis=0
    )


def kernel(
    upto,
    geno, covh, pheh, permh, winh,
    cur_ref, peak_ref,
    perm, win, xc, xy, xp, gs, gg, pk, gm, gcp, gr, ga, gh, yt, tab, yo, ds,
    pq, pr, q0, s0, rb, sb, xs, xm, fm,
    in_sem, geno_sem, g1_s, g1_r, p_s, p_r, pk_s, pk_r, c_s, c_r, f_s, f_r, h_s, h_r,
    gr_s, gr_r, ga_s, ga_r, gh_s, gh_r, t_s, t_r, y_s, y_r,
    pr_s, pr_r, rs_s, rs_r, x_s, x_r, o_s, o_r,
):
    s = lax.axis_index("samp")
    b = lax.axis_index("var")
    z = lax.div(s, 2)
    c = lax.rem(s, 2)
    oc = 1 - c
    up_band = lax.rem(b + 1, NB)
    down_band = lax.rem(b + NB - 1, NB)
    nbr = lax.rem(b + 2 * c - 1 + NB, NB)
    own_at = pl.multiple_of(oc * VH, VH)
    halo_at = pl.multiple_of(c * VH, VH)

    def zc(k):
        return lax.rem(z + k % NZ, NZ)

    def dev(zz, cc, bb):
        return {"samp": zz * 2 + cc, "var": bb}

    def half(cc):
        return pl.ds(pl.multiple_of(cc * VH, VH), VH)

    sent, due = [], {}

    def start(key, src, dst, ss, rs, to, here, here_sem):
        d = pltpu.make_async_remote_copy(
            src_ref=src, dst_ref=dst, send_sem=ss, recv_sem=rs, device_id=to, device_id_type=MESH
        )
        d.start()
        sent.append(d)
        due[key] = (here, here_sem)

    def landed(key):
        here, sem = due.pop(key)
        pltpu.make_async_remote_copy(
            src_ref=here, dst_ref=here, send_sem=sem, recv_sem=sem,
            device_id=dev(z, oc, b), device_id_type=MESH,
        ).wait_recv()

    def stop():
        for key in list(due):
            landed(key)
        for d in sent:
            d.wait_send()

    def cut(level):
        if upto != level:
            return False
        stop()
        cur_ref[...] = jnp.zeros_like(cur_ref)
        peak_ref[...] = jnp.zeros_like(peak_ref)
        return True

    other = dev(z, oc, b)
    loads = [
        pltpu.make_async_copy(src, dst, in_sem.at[i])
        for i, (src, dst) in enumerate((
            (covh, xc.at[z]), (pheh, xy.at[z]), (permh, perm), (winh, win),
        ))
    ]
    for d in loads:
        d.start()
    barrier = pltpu.get_barrier_semaphore()
    peers = [dev(zc(k), c, b) for k in range(1, NZ)] + [other]
    peers += [dev(z, cc, bb) for cc in (0, 1) for bb in (up_band, down_band)]
    for peer in peers:
        pl.semaphore_signal(barrier, inc=1, device_id=peer, device_id_type=MESH)
    own_geno = pltpu.make_async_copy(geno.at[:, half(c)], gs.at[c, :, pl.ds(own_at, VH)], geno_sem)
    own_geno.start()
    for d in loads:
        d.wait()

    phe = xy[z]
    full = jnp.concatenate([phe, phe], axis=0)
    hi = full.astype(BF16).astype(F32)
    rest = full - hi
    mid = rest.astype(BF16).astype(F32)
    low = (rest - mid).astype(BF16).astype(F32)
    row8 = iota((8, NS), 0)
    block_a = jnp.where(row8 < 4, hi, mid)
    block_b = jnp.where(row8 < 4, low, jnp.where(row8 == 4, 1.0, 0.0))
    xp[c] = jnp.concatenate([xc[z].astype(F32), block_a, block_b], axis=0).astype(BF16)
    mine = xp[c]
    gg[c] = jnp.zeros((GR, 128), F32)
    gg[c, :, 0:XR] = fold_rows(nt(mine, mine))

    pl.semaphore_wait(barrier, len(peers))
    start("g1", gg.at[c], gg.at[c], g1_s, g1_r, other, gg.at[oc], g1_r)
    start("p", xp.at[c], xp.at[c], p_s, p_r, other, xp.at[oc], p_r)
    if cut(0):
        own_geno.wait()
        return

    landed("g1")
    g = gg[0] + gg[1]
    lane40 = iota((GR, 128), 1)
    g = jnp.where(lane40 < GONE, g, pltpu.roll(g, 128 - (ONE - GONE), axis=1))
    g = jnp.concatenate([g, jnp.zeros((8, 128), F32)], axis=0)
    lane16 = iota((16, 128), 1)
    pk[z] = jnp.where(
        lane16 < GR, g[0:16],
        jnp.where(lane16 < 2 * GR, pltpu.roll(g[16:32], GR, axis=1),
                  jnp.where(lane16 < 3 * GR, pltpu.roll(g[32:48], 2 * GR, axis=1), 0.0)),
    )
    near = (1, 7, 2, 6, 3, 5, 4)
    for k in near:
        start(("pk", k), pk.at[z], pk.at[z], pk_s.at[k], pk_r.at[NZ - k], dev(zc(k), c, b),
              pk.at[zc(k)], pk_r.at[k])
    start("f", geno.at[:, half(oc)], gs.at[c, :, half(c)], f_s, f_r, other,
          gs.at[oc, :, pl.ds(own_at, VH)], f_r)

    def share(name, held, to):
        ref = (xc, xy)[name == "y"]
        i, k, got = int(name == "y"), (held - to) % NZ, zc(held - to)
        start((name, k), ref.at[zc(held)], ref.at[zc(held)], c_s.at[i, k], c_r.at[i, k],
              dev(zc(to), c, b), ref.at[got], c_r.at[i, k])

    for to in (1, -1, 2, -2):
        share("c", 0, to)
        share("y", 0, to)
    halo = gs.at[0, :, pl.ds(halo_at, VH)], gs.at[1, :, pl.ds(halo_at, VH)]
    start("h0", geno.at[:, VH:2 * VH], gs.at[c, :, 0:VH], h_s.at[0], h_r.at[c],
          dev(z, 0, up_band), halo[0], h_r.at[0])
    start("h1", geno.at[:, 0:VH], gs.at[c, :, VH:2 * VH], h_s.at[1], h_r.at[c],
          dev(z, 1, down_band), halo[1], h_r.at[1])

    own_geno.wait()
    landed("f")
    landed("p")
    gpart = fold_rows(
        mm(xp[0], gs[0, :, pl.ds(own_at, VH)]) + mm(xp[1], gs[1, :, pl.ds(own_at, VH)])
    )
    for name in ("c", "y"):
        for k in (6, 2):
            landed((name, k))
    share("c", -2, 2)
    share("y", 2, -2)
    for name in ("c", "y"):
        share(name, -2, 1)
        share(name, 2, -1)
    mean = gpart[GONE:GONE + 1, :] * (1.0 / (2 * NS))

    def spread(i, acc):
        at = pl.ds(pl.multiple_of(lax.rem(i, 32) * 16, 16), 16)
        dif = gs[lax.div(i, 32), at, pl.ds(own_at, VH)].astype(F32) - mean
        return acc + dif * dif

    acc = lax.fori_loop(0, 64, spread, jnp.zeros((16, VH), F32))
    rowg = iota((GR, VH), 0)
    gpart = jnp.where(rowg == GSP, jnp.sum(acc, axis=0, keepdims=True), gpart)
    for j in range(NZ):
        gcp[j] = gpart[:, j * 128:(j + 1) * 128]
    for k in near:
        start(("gr", k), gcp.at[zc(k)], gr.at[z], gr_s.at[k], gr_r.at[NZ - k], dev(zc(k), c, b),
              gr.at[zc(k)], gr_r.at[k])

    for k in range(1, NZ):
        landed(("pk", k))
    if cut(1):
        return
    tot = pk[0]
    for j in range(1, NZ):
        tot = tot + pk[j]
    a = jnp.concatenate(
        [tot, pltpu.roll(tot, 128 - GR, axis=1), pltpu.roll(tot, 128 - 2 * GR, axis=1)[0:8]], axis=0
    )
    row, lane = iota((GR, 128), 0), iota((GR, 128), 1)
    in_row = (row < NC) | (row == GONE)
    in_lane = (lane < NC) | (lane == GONE)
    a = jnp.where(in_lane, a, 0.0)
    colmean = a[:, GONE:GONE + 1] * (1.0 / NSAMP)
    for k in (GONE,) + tuple(range(NC)):
        q = a[:, k:k + 1]
        r = a[k:k + 1, :]
        inv = 1.0 / a[k:k + 1, k:k + 1]
        rr = r * inv
        nxt = a - q * rr
        nxt = jnp.where(row == k, rr, nxt)
        nxt = jnp.where(lane == k, jnp.where(row == k, -inv, q * inv), nxt)
        a = nxt
    gm[...] = jnp.where(in_row & in_lane, -a, 0.0)

    beta = a[32:40, :]
    row24 = beta.astype(BF16).astype(F32)
    rest = beta - row24
    mid = rest.astype(BF16).astype(F32)
    coefs = jnp.concatenate([row24, mid, rest - mid], axis=0)[:, 0:NC].astype(BF16)
    const = beta[0:4, GONE:GONE + 1]
    if cut(2):
        return
    for k in (0, 7, 1, 6, 2, 5, 3, 4):
        for name in ("c", "y"):
            if (name, k) in due:
                landed((name, k))
        t = mm(coefs, xc[zc(k)])
        fit = (t[16:24] + t[8:16]) + t[0:8]
        yt[c, zc(k)] = xy[zc(k)] - (fit[0:4] + const)
    start("t", yt.at[c], yt.at[c], t_s, t_r, other, yt.at[oc], t_r)

    landed("t")
    ysq = jnp.zeros((NG, NS), F32)
    for cc in range(2):
        for j in range(NZ):
            ysq = ysq + yt[cc, j] * yt[cc, j]
    ynorm = jnp.sqrt(jnp.sum(ysq, axis=1, keepdims=True) + EPS)
    for cc in range(2):
        for j in range(NZ):
            y = yt[cc, j] / ynorm
            for q in range(2):
                at = (2 * (2 * j + cc) + q) * NG
                tab[at:at + NG, :] = y[:, q * LO:(q + 1) * LO]
    if cut(3):
        return

    table = tab[...].astype(BF16)
    count = iota((LO, NS), 0).astype(F32).astype(BF16)
    holds = lax.shift_right_logical(iota((TR, NS), 0), 2)
    low_half = iota((8, NS), 0) < NG
    one = jnp.ones((), BF16)
    zero = jnp.zeros((), BF16)

    def look(i, carry):
        got = []
        for u in range(4):
            idx = perm[pl.ds(i * 4 + u, 1), :]
            ilo = lax.bitwise_and(idx, LO - 1).astype(F32).astype(BF16)
            found = mm(table, jnp.where(count == ilo, one, zero))
            found = jnp.where(holds == lax.shift_right_logical(idx, 8), found, 0.0)
            part = found[0:8]
            for j in range(1, TR // 8):
                part = part + found[j * 8:(j + 1) * 8]
            got.append(part + pltpu.roll(part, NG, axis=0))
        rows = jnp.concatenate(
            [jnp.where(low_half, got[0], got[1]), jnp.where(low_half, got[2], got[3])], axis=0
        )
        yo[c, pl.ds(pl.multiple_of(i * 16, 16), 16), :] = rows.astype(BF16)
        return carry

    def sum_variants():
        for k in range(1, NZ):
            landed(("gr", k))
        gr[z] = gcp[z]
        tot = gr[0]
        for j in range(1, NZ):
            tot = tot + gr[j]
        mu = tot[GONE:GONE + 1, :] * (1.0 / NSAMP)
        between = jnp.zeros((1, 128), F32)
        for j in range(NZ):
            off = gr[j, GONE:GONE + 1, :] * (1.0 / (2 * NS)) - mu
            between = between + off * off
        ga[z] = tot + jnp.where(row == GSP, between * (2.0 * NS), 0.0)
        for k in near:
            start(("ga", k), ga.at[z], ga.at[z], ga_s.at[k], ga_r.at[NZ - k], dev(zc(k), c, b),
                  ga.at[zc(k)], ga_r.at[k])

    for j in range(3):
        lax.fori_loop(j * 4, j * 4 + 4, look, 0)
        part = pl.ds(j * 64, 64)
        start(("yo", j), yo.at[c, part], yo.at[c, part], y_s.at[j], y_r.at[j], other,
              yo.at[oc, part], y_r.at[j])
        if j == 0:
            sum_variants()
    if cut(4):
        return
    for j in range(3):
        landed(("yo", j))

    def product(kind, at):
        ds[kind] = mm(yo[0], gs[0, :, pl.ds(at, VH)]) + mm(yo[1], gs[1, :, pl.ds(at, VH)])

    def chunk(kind, k):
        return ds.at[kind, pl.ds(pl.multiple_of(zc(k) * CH, CH), CH)]

    def hops(kind, way):
        return HOPS[(kind + way) % 2]

    def unpack(ref, scale):
        q = ref[...].astype(F32)
        return [q[CH * h:CH * (h + 1)] * scale[h:h + 1, :] for h in range(2)]

    def halves(ref):
        return [ref[:, HW * h:HW * (h + 1)] for h in range(2)]

    def send_sum(kind, way, t):
        n = hops(kind, way)
        sign = 1 - 2 * way
        parts = halves(chunk(kind, -sign * (n - t)))
        if t == 0:
            src, scale = q0.at[kind, way], s0.at[kind, way]
        else:
            src, scale = rb.at[kind, way, t - 1], sb.at[kind, way, t - 1]
            landed(("rs", kind, way, t - 1))
            landed(("sc", kind, way, t - 1))
            parts = [u + v for u, v in zip(parts, unpack(src, scale))]
        codes = []
        for h in range(2):
            top = jnp.max(jnp.abs(parts[h]), axis=0, keepdims=True)
            top = jnp.maximum(top, TINY)
            scale[h:h + 1, :] = top * (1.0 / QMAX)
            codes.append(jnp.round(parts[h] * (QMAX / top)))
        src[...] = jnp.concatenate(codes, axis=0).astype(jnp.int32).astype(jnp.int16)
        to = dev(zc(-sign), c, b)
        for i, (name, here, buf) in enumerate((("rs", src, rb), ("sc", scale, sb))):
            land = buf.at[kind, way, t]
            start((name, kind, way, t), here, land, rs_s.at[i, kind, way, t],
                  rs_r.at[i, kind, way, t], to, land, rs_r.at[i, kind, way, t])

    proj = jnp.concatenate(
        [nt(yo[0], xp[0]) + nt(yo[1], xp[1]), jnp.zeros((ROWS, 128 - XR), F32)], axis=1
    )
    proj = jnp.where(iota((ROWS, 128), 1) < GONE, proj, pltpu.roll(proj, 128 - (ONE - GONE), axis=1))
    lane8 = iota((8, 128), 1)
    for j in range(NZ):
        p3 = [proj[CH * j + 8 * i:CH * j + 8 * i + 8] for i in range(3)]
        pq[j] = jnp.where(
            lane8 < GR, p3[0],
            jnp.where(lane8 < 2 * GR, pltpu.roll(p3[1], GR, axis=1),
                      pltpu.roll(p3[2], 2 * GR, axis=1)),
        )
    product(0, own_at)
    send_sum(0, 0, 0)
    send_sum(0, 1, 0)
    landed("h0")
    landed("h1")
    product(1, halo_at)
    send_sum(1, 1, 0)
    send_sum(1, 0, 0)
    for k in near:
        start(("pr", k), pq.at[zc(k)], pr.at[z], pr_s.at[k], pr_r.at[NZ - k], dev(zc(k), c, b),
              pr.at[zc(k)], pr_r.at[k])
    if cut(5):
        return

    for k in range(1, NZ):
        landed(("ga", k))
    start("gh", ga, gh, gh_s, gh_r, dev(z, oc, nbr), gh, gh_r)

    inv = gm[:, 0:GR]

    def of_variants(ref):
        gx = jnp.concatenate([ref[j] for j in range(NZ)], axis=1)
        centred = jnp.where(rowg < NC, gx - colmean * gx[GONE:GONE + 1, :], 0.0)
        explained = jnp.sum(centred * mm(inv, centred, HIGH), axis=0, keepdims=True)
        weight = 1.0 / (jnp.maximum(gx[GSP:GSP + 1, :] - explained, 0.0) + EPS)
        return mm(inv, jnp.where((rowg < NC) | (rowg == GONE), gx, 0.0), HIGH), weight

    beta_own, weight_own = of_variants(ga)
    order = ((0, 0), (0, 1), (1, 1), (1, 0))
    for kind, way in order:
        send_sum(kind, way, 1)
    landed("gh")
    beta_halo, weight_halo = of_variants(gh)
    for t in range(2, 4):
        for kind, way in order:
            if t < hops(kind, way):
                send_sum(kind, way, t)

    gene24 = lax.rem(iota((CH, 1), 0), NG)
    first = jnp.zeros((CH, 1), jnp.int32)
    last = jnp.zeros((CH, 1), jnp.int32)
    for g in range(NG):
        first = jnp.where(gene24 == g, win[0, b * NG + g], first)
        last = jnp.where(gene24 == g, win[1, b * NG + g], last)
    base = b * VB - VH + c * VB + iota((CH, VH), 1)

    for k in range(1, NZ):
        landed(("pr", k))
    pr[z] = pq[z]
    tot = pr[0]
    for j in range(1, NZ):
        tot = tot + pr[j]
    proj = jnp.concatenate(
        [tot, pltpu.roll(tot, 128 - GR, axis=1), pltpu.roll(tot, 128 - 2 * GR, axis=1)], axis=0
    )
    l24 = iota((CH, 128), 1)
    proj = jnp.where((l24 < NC) | (l24 == GONE), proj, 0.0)[:, 0:GR]

    sums = []
    for kind in range(2):
        parts = halves(chunk(kind, 0))
        for way in range(2):
            end = hops(kind, way) - 1
            landed(("rs", kind, way, end))
            landed(("sc", kind, way, end))
            got = unpack(rb.at[kind, way, end], sb.at[kind, way, end])
            parts = [u + v for u, v in zip(parts, got)]
        sums.append(jnp.concatenate(parts, axis=1))
    if cut(6):
        return

    def largest(kind, at, beta_g, weight):
        numer = sums[kind] - mm(proj, beta_g, HIGH)
        pos = base + at
        inside = (pos >= first) & (pos < last)
        return jnp.max(jnp.where(inside, numer * numer * weight, 0.0), axis=1, keepdims=True)

    best = jnp.maximum(
        largest(0, own_at, beta_own, weight_own), largest(1, halo_at, beta_halo, weight_halo)
    )
    xs[...] = jnp.broadcast_to(best, (CH, 128))
    start("x", xs, xm, x_s, x_r, other, xm, x_r)
    landed("x")
    best = jnp.maximum(xs[...], xm[...]) * float(NSAMP)

    r24, l24 = iota((CH, 128), 0), iota((CH, 128), 1)
    placed = jnp.where(l24 == lax.shift_right_logical(r24, 2) + PZ * z, best, 0.0)
    level = LEVMAX * l24.astype(F32) / (LEVELS - 1)
    curve = jax.nn.sigmoid(best - level)

    def over_perms(v):
        v = (v[0:8] + v[8:16]) + v[16:24]
        return v + pltpu.roll(v, NG, axis=0)

    fm[z] = jnp.where(iota((8, 128), 0) < NG, over_perms(placed), over_perms(curve))
    for k in near:
        start(("o", k), fm.at[z], fm.at[z], o_s.at[k], o_r.at[NZ - k], dev(zc(k), c, b),
              fm.at[zc(k)], o_r.at[k])
    for k in range(1, NZ):
        landed(("o", k))
    both = fm[0]
    for j in range(1, NZ):
        both = both + fm[j]
    peak_ref[...] = both[0:NG, 0:NP]
    cur_ref[...] = both[NG:2 * NG, 0:LEVELS] * (1.0 / NP)
    stop()


def per_device(upto, geno, covar, pheno, perm, windows):
    dma = pltpu.SemaphoreType.DMA
    vmem = pltpu.VMEM
    spec = pl.BlockSpec(memory_space=pltpu.VMEM)
    return pl.pallas_call(
        functools.partial(kernel, upto),
        out_shape=(
            jax.ShapeDtypeStruct((NG, LEVELS), F32),
            jax.ShapeDtypeStruct((NG, NP), F32),
        ),
        in_specs=[pl.BlockSpec(memory_space=pltpu.HBM)] * 5,
        out_specs=(spec, spec),
        scratch_shapes=[
            vmem((NP, NS), jnp.int32),
            pltpu.SMEM((2, NG * NB), jnp.int32),
            vmem((NZ, NC, NS), BF16),
            vmem((NZ, NG, NS), F32),
            vmem((2, XR, NS), BF16),
            vmem((2, NS, VB), BF16),
            vmem((2, GR, 128), F32),
            vmem((NZ, 16, 128), F32),
            vmem((GR, 128), F32),
            vmem((NZ, GR, 128), F32),
            vmem((NZ, GR, 128), F32),
            vmem((NZ, GR, 128), F32),
            vmem((NZ, GR, 128), F32),
            vmem((2, NZ, NG, NS), F32),
            vmem((TR, LO), F32),
            vmem((2, ROWS, NS), BF16),
            vmem((2, ROWS, VH), F32),
            vmem((NZ, 8, 128), F32),
            vmem((NZ, 8, 128), F32),
            vmem((2, 2, 2 * CH, HW), jnp.int16),
            vmem((2, 2, 2, HW), F32),
            vmem((2, 2, 4, 2 * CH, HW), jnp.int16),
            vmem((2, 2, 4, 2, HW), F32),
            vmem((CH, 128), F32),
            vmem((CH, 128), F32),
            vmem((NZ, 8, 128), F32),
            dma((4,)), dma,
            dma, dma, dma, dma,
            dma((NZ,)), dma((NZ,)),
            dma((2, NZ)), dma((2, NZ)),
            dma, dma,
            dma((2,)), dma((2,)),
            dma((NZ,)), dma((NZ,)),
            dma((NZ,)), dma((NZ,)),
            dma, dma, dma, dma,
            dma((3,)), dma((3,)),
            dma((NZ,)), dma((NZ,)),
            dma((2, 2, 2, 4)), dma((2, 2, 2, 4)),
            dma, dma,
            dma((NZ,)), dma((NZ,)),
        ],
        compiler_params=pltpu.CompilerParams(
            collective_id=0, has_side_effects=True, vmem_limit_bytes=56 * 1024 * 1024
        ),
        name="scan",
    )(geno, covar.T, pheno.T, perm, windows.T)


def build(mesh, upto):
    in_specs = (P("samp", "var"), P("samp", None), P("samp", "var"), P(None, "samp"), P())
    out_specs = (P("var", None), P("var", None))
    return jax.shard_map(
        functools.partial(per_device, upto), mesh=mesh, in_specs=in_specs, out_specs=out_specs,
        check_vma=False,
    )


def solution(mesh):
    return build(mesh, 9)
```

```python
import functools

import jax
import jax.numpy as jnp
from jax import lax
from jax.experimental import pallas as pl
from jax.experimental.pallas import tpu as pltpu
from jax.sharding import PartitionSpec as P

MESH = pl.DeviceIdType.MESH
F32 = jnp.float32
BF16 = jnp.bfloat16
HIGH = lax.Precision.HIGHEST

EPS = 1e-06
LEVMAX = 40.0
LEVELS = 64

NZ = 8
NB = 16
NS = 512
NSAMP = 8192
VB = 2048
VH = 1024
NG = 4
NP = 48
NC = 32
XR = 48
ONE = 44
SPARE = 45
GR = 40
GONE = 36
GSP = 37
ROWS = NG * NP
CH = ROWS // NZ
HW = VH // 2
QMAX = 32767.0
TINY = 1e-30
HOPS = (4, 3)
LO = 256
TR = NSAMP // LO * NG
PZ = NP // NZ


def nt(a, b):
    return lax.dot_general(a, b, (((1,), (1,)), ((), ())), preferred_element_type=F32)


def mm(a, b, precision=None):
    return lax.dot_general(
        a, b, (((1,), (0,)), ((), ())), preferred_element_type=F32, precision=precision
    )


def iota(shape, dim):
    return lax.broadcasted_iota(jnp.int32, shape, dim)


def fold_rows(v):
    head, body, tail = v[0:32], v[32:40], v[40:48]
    low = iota(body.shape, 0) < 4
    return jnp.concatenate(
        [head, jnp.where(low, body + pltpu.roll(body, 4, axis=0) + tail, tail)], axis=0
    )


def kernel(
    upto,
    geno, covh, pheh, permh, winh,
    out_ref,
    perm, win, xc, xy, xp, gs, gg, pk, gm, gcp, gr, ga, gh, yt, tab, yo, ds,
    pq, pr, q0, s0, rb, sb, wm, fm,
    in_sem, geno_sem, g1_s, g1_r, p_s, p_r, pk_s, pk_r, c_s, c_r, f_s, f_r, h_s, h_r,
    gr_s, gr_r, ga_s, ga_r, gh_s, gh_r, t_s, t_r, y_s, y_r,
    pr_s, pr_r, rs_s, rs_r, o_s, o_r,
):
    s = lax.axis_index("samp")
    b = lax.axis_index("var")
    z = lax.div(s, 2)
    c = lax.rem(s, 2)
    oc = 1 - c
    up_band = lax.rem(b + 1, NB)
    down_band = lax.rem(b + NB - 1, NB)
    nbr = lax.rem(b + 2 * c - 1 + NB, NB)
    own_at = pl.multiple_of(oc * VH, VH)
    halo_at = pl.multiple_of(c * VH, VH)

    def zc(k):
        return lax.rem(z + k % NZ, NZ)

    def dev(zz, cc, bb):
        return {"samp": zz * 2 + cc, "var": bb}

    def half(cc):
        return pl.ds(pl.multiple_of(cc * VH, VH), VH)

    sent, due = [], {}

    def start(key, src, dst, ss, rs, to, here, here_sem):
        d = pltpu.make_async_remote_copy(
            src_ref=src, dst_ref=dst, send_sem=ss, recv_sem=rs, device_id=to, device_id_type=MESH
        )
        d.start()
        sent.append(d)
        due[key] = (here, here_sem)

    def landed(key):
        here, sem = due.pop(key)
        pltpu.make_async_remote_copy(
            src_ref=here, dst_ref=here, send_sem=sem, recv_sem=sem,
            device_id=dev(z, oc, b), device_id_type=MESH,
        ).wait_recv()

    def stop():
        for key in list(due):
            landed(key)
        for d in sent:
            d.wait_send()

    def cut(level):
        if upto != level:
            return False
        stop()
        out_ref[...] = jnp.zeros_like(out_ref)
        return True

    other = dev(z, oc, b)
    loads = [
        pltpu.make_async_copy(src, dst, in_sem.at[i])
        for i, (src, dst) in enumerate((
            (covh, xc.at[z]), (pheh, xy.at[z]), (permh, perm), (winh, win),
        ))
    ]
    for d in loads:
        d.start()
    barrier = pltpu.get_barrier_semaphore()
    peers = [dev(zc(k), cc, b) for k in range(1, NZ) for cc in (0, 1)] + [other]
    peers += [dev(z, cc, bb) for cc in (0, 1) for bb in (up_band, down_band)]
    for peer in peers:
        pl.semaphore_signal(barrier, inc=1, device_id=peer, device_id_type=MESH)
    own_geno = pltpu.make_async_copy(geno.at[:, half(c)], gs.at[c, :, pl.ds(own_at, VH)], geno_sem)
    own_geno.start()
    for d in loads:
        d.wait()

    phe = xy[z]
    full = jnp.concatenate([phe, phe], axis=0)
    hi = full.astype(BF16).astype(F32)
    rest = full - hi
    mid = rest.astype(BF16).astype(F32)
    low = (rest - mid).astype(BF16).astype(F32)
    row8 = iota((8, NS), 0)
    block_a = jnp.where(row8 < 4, hi, mid)
    block_b = jnp.where(row8 < 4, low, jnp.where(row8 == 4, 1.0, 0.0))
    xp[c] = jnp.concatenate([xc[z].astype(F32), block_a, block_b], axis=0).astype(BF16)
    mine = xp[c]
    gg[c] = jnp.zeros((GR, 128), F32)
    gg[c, :, 0:XR] = fold_rows(nt(mine, mine))

    pl.semaphore_wait(barrier, len(peers))
    start("g1", gg.at[c], gg.at[c], g1_s, g1_r, other, gg.at[oc], g1_r)
    start("p", xp.at[c], xp.at[c], p_s, p_r, other, xp.at[oc], p_r)

    halo = gs.at[0, :, pl.ds(halo_at, VH)], gs.at[1, :, pl.ds(halo_at, VH)]
    start("h0", geno.at[:, VH:2 * VH], gs.at[c, :, 0:VH], h_s.at[0], h_r.at[c],
          dev(z, 0, up_band), halo[0], h_r.at[0])
    start("h1", geno.at[:, 0:VH], gs.at[c, :, VH:2 * VH], h_s.at[1], h_r.at[c],
          dev(z, 1, down_band), halo[1], h_r.at[1])
    if cut(0):
        own_geno.wait()
        return

    landed("g1")
    g = gg[0] + gg[1]
    lane40 = iota((GR, 128), 1)
    g = jnp.where(lane40 < GONE, g, pltpu.roll(g, 128 - (ONE - GONE), axis=1))
    g = jnp.concatenate([g, jnp.zeros((8, 128), F32)], axis=0)
    lane16 = iota((16, 128), 1)
    pk[z] = jnp.where(
        lane16 < GR, g[0:16],
        jnp.where(lane16 < 2 * GR, pltpu.roll(g[16:32], GR, axis=1),
                  jnp.where(lane16 < 3 * GR, pltpu.roll(g[32:48], 2 * GR, axis=1), 0.0)),
    )
    near = (1, 7, 2, 6, 3, 5, 4)
    for k in near:
        start(("pk", k), pk.at[z], pk.at[z], pk_s.at[k], pk_r.at[NZ - k], dev(zc(k), c, b),
              pk.at[zc(k)], pk_r.at[k])
    start("f", geno.at[:, half(oc)], gs.at[c, :, half(c)], f_s, f_r, other,
          gs.at[oc, :, pl.ds(own_at, VH)], f_r)

    def share(name, held, to):
        ref = (xc, xy)[name == "y"]
        i, k, got = int(name == "y"), (held - to) % NZ, zc(held - to)
        start((name, k), ref.at[zc(held)], ref.at[zc(held)], c_s.at[i, k], c_r.at[i, k],
              dev(zc(to), c, b), ref.at[got], c_r.at[i, k])

    for to in (1, -1, 2, -2):
        share("c", 0, to)
        share("y", 0, to)
    own_geno.wait()
    landed("f")
    landed("p")
    gpart = fold_rows(
        mm(xp[0], gs[0, :, pl.ds(own_at, VH)]) + mm(xp[1], gs[1, :, pl.ds(own_at, VH)])
    )
    for name in ("c", "y"):
        for k in (6, 2):
            landed((name, k))
    share("c", -2, 2)
    share("y", 2, -2)
    for name in ("c", "y"):
        share(name, -2, 1)
        share(name, 2, -1)
    mean = gpart[GONE:GONE + 1, :] * (1.0 / (2 * NS))

    def spread(i, acc):
        at = pl.ds(pl.multiple_of(lax.rem(i, 32) * 16, 16), 16)
        dif = gs[lax.div(i, 32), at, pl.ds(own_at, VH)].astype(F32) - mean
        return acc + dif * dif

    acc = lax.fori_loop(0, 64, spread, jnp.zeros((16, VH), F32), unroll=4)
    rowg = iota((GR, VH), 0)
    gpart = jnp.where(rowg == GSP, jnp.sum(acc, axis=0, keepdims=True), gpart)
    for j in range(NZ):
        gcp[j] = gpart[:, j * 128:(j + 1) * 128]
    for k in near:
        start(("gr", k), gcp.at[zc(k)], gr.at[z], gr_s.at[k], gr_r.at[NZ - k], dev(zc(k), c, b),
              gr.at[zc(k)], gr_r.at[k])

    for k in range(1, NZ):
        landed(("pk", k))
    if cut(1):
        return
    tot = pk[0]
    for j in range(1, NZ):
        tot = tot + pk[j]
    a = jnp.concatenate(
        [tot, pltpu.roll(tot, 128 - GR, axis=1), pltpu.roll(tot, 128 - 2 * GR, axis=1)[0:8]], axis=0
    )
    row, lane = iota((GR, 128), 0), iota((GR, 128), 1)
    in_row = (row < NC) | (row == GONE)
    in_lane = (lane < NC) | (lane == GONE)
    a = jnp.where(in_lane, a, 0.0)
    colmean = a[:, GONE:GONE + 1] * (1.0 / NSAMP)
    for k in (GONE,) + tuple(range(NC)):
        q = a[:, k:k + 1]
        r = a[k:k + 1, :]
        inv = 1.0 / a[k:k + 1, k:k + 1]
        rr = r * inv
        nxt = a - q * rr
        nxt = jnp.where(row == k, rr, nxt)
        nxt = jnp.where(lane == k, jnp.where(row == k, -inv, q * inv), nxt)
        a = nxt
    gm[...] = jnp.where(in_row & in_lane, -a, 0.0)

    beta = a[32:40, :]
    row24 = beta.astype(BF16).astype(F32)
    rest = beta - row24
    mid = rest.astype(BF16).astype(F32)
    coefs = jnp.concatenate([row24, mid, rest - mid], axis=0)[:, 0:NC].astype(BF16)
    const = beta[0:4, GONE:GONE + 1]
    if cut(2):
        return
    for k in (0, 7, 1, 6, 2, 5, 3, 4):
        for name in ("c", "y"):
            if (name, k) in due:
                landed((name, k))
        t = mm(coefs, xc[zc(k)])
        fit = (t[16:24] + t[8:16]) + t[0:8]
        yt[c, zc(k)] = xy[zc(k)] - (fit[0:4] + const)
    start("t", yt.at[c], yt.at[c], t_s, t_r, other, yt.at[oc], t_r)

    landed("t")
    ysq = jnp.zeros((NG, NS), F32)
    for cc in range(2):
        for j in range(NZ):
            ysq = ysq + yt[cc, j] * yt[cc, j]
    ynorm = jnp.sqrt(jnp.sum(ysq, axis=1, keepdims=True) + EPS)
    for cc in range(2):
        for j in range(NZ):
            y = yt[cc, j] / ynorm
            for q in range(2):
                at = (2 * (2 * j + cc) + q) * NG
                tab[at:at + NG, :] = y[:, q * LO:(q + 1) * LO]
    if cut(3):
        return

    table = tab[...].astype(BF16)
    count = iota((LO, NS), 0).astype(F32).astype(BF16)
    holds = lax.shift_right_logical(iota((TR, NS), 0), 2)
    low_half = iota((8, NS), 0) < NG
    one = jnp.ones((), BF16)
    zero = jnp.zeros((), BF16)

    def look(i, carry):
        got = []
        for u in range(4):
            idx = perm[pl.ds(i * 4 + u, 1), :]
            ilo = lax.bitwise_and(idx, LO - 1).astype(F32).astype(BF16)
            found = mm(table, jnp.where(count == ilo, one, zero))
            found = jnp.where(holds == lax.shift_right_logical(idx, 8), found, 0.0)
            part = found[0:8]
            for j in range(1, TR // 8):
                part = part + found[j * 8:(j + 1) * 8]
            got.append(part + pltpu.roll(part, NG, axis=0))
        rows = jnp.concatenate(
            [jnp.where(low_half, got[0], got[1]), jnp.where(low_half, got[2], got[3])], axis=0
        )
        yo[c, pl.ds(pl.multiple_of(i * 16, 16), 16), :] = rows.astype(BF16)
        return carry

    def sum_variants():
        for k in range(1, NZ):
            landed(("gr", k))
        gr[z] = gcp[z]
        tot = gr[0]
        for j in range(1, NZ):
            tot = tot + gr[j]
        mu = tot[GONE:GONE + 1, :] * (1.0 / NSAMP)
        between = jnp.zeros((1, 128), F32)
        for j in range(NZ):
            off = gr[j, GONE:GONE + 1, :] * (1.0 / (2 * NS)) - mu
            between = between + off * off
        ga[z] = tot + jnp.where(row == GSP, between * (2.0 * NS), 0.0)
        for k in near:
            start(("ga", k), ga.at[z], ga.at[z], ga_s.at[k], ga_r.at[NZ - k], dev(zc(k), c, b),
                  ga.at[zc(k)], ga_r.at[k])

    for j in range(3):
        lax.fori_loop(j * 4, j * 4 + 4, look, 0)
        part = pl.ds(j * 64, 64)
        start(("yo", j), yo.at[c, part], yo.at[c, part], y_s.at[j], y_r.at[j], other,
              yo.at[oc, part], y_r.at[j])
        if j == 0:
            sum_variants()
    if cut(4):
        return
    for j in range(3):
        landed(("yo", j))

    def product(kind, at):
        ds[kind] = mm(yo[0], gs[0, :, pl.ds(at, VH)]) + mm(yo[1], gs[1, :, pl.ds(at, VH)])

    def chunk(kind, k):
        return ds.at[kind, pl.ds(pl.multiple_of(zc(k) * CH, CH), CH)]

    def hops(kind, way):
        return HOPS[(kind + way) % 2]

    def unpack(ref, scale):
        q = ref[...].astype(F32)
        return [q[CH * h:CH * (h + 1)] * scale[h:h + 1, :] for h in range(2)]

    def halves(ref):
        return [ref[:, HW * h:HW * (h + 1)] for h in range(2)]

    def send_sum(kind, way, t):
        n = hops(kind, way)
        sign = 1 - 2 * way
        parts = halves(chunk(kind, -sign * (n - t)))
        if t == 0:
            src, scale = q0.at[kind, way], s0.at[kind, way]
        else:
            src, scale = rb.at[kind, way, t - 1], sb.at[kind, way, t - 1]
            landed(("rs", kind, way, t - 1))
            landed(("sc", kind, way, t - 1))
            parts = [u + v for u, v in zip(parts, unpack(src, scale))]
        codes = []
        for h in range(2):
            top = jnp.max(jnp.abs(parts[h]), axis=0, keepdims=True)
            top = jnp.maximum(top, TINY)
            scale[h:h + 1, :] = top * (1.0 / QMAX)
            codes.append(jnp.round(parts[h] * (QMAX / top)))
        src[...] = jnp.concatenate(codes, axis=0).astype(jnp.int32).astype(jnp.int16)
        to = dev(zc(-sign), c, b)
        for i, (name, here, buf) in enumerate((("rs", src, rb), ("sc", scale, sb))):
            land = buf.at[kind, way, t]
            start((name, kind, way, t), here, land, rs_s.at[i, kind, way, t],
                  rs_r.at[i, kind, way, t], to, land, rs_r.at[i, kind, way, t])

    product(0, own_at)
    send_sum(0, 0, 0)
    send_sum(0, 1, 0)

    proj = jnp.concatenate(
        [nt(yo[0], xp[0]) + nt(yo[1], xp[1]), jnp.zeros((ROWS, 128 - XR), F32)], axis=1
    )
    proj = jnp.where(iota((ROWS, 128), 1) < GONE, proj, pltpu.roll(proj, 128 - (ONE - GONE), axis=1))
    lane8 = iota((8, 128), 1)
    for j in range(NZ):
        p3 = [proj[CH * j + 8 * i:CH * j + 8 * i + 8] for i in range(3)]
        pq[j] = jnp.where(
            lane8 < GR, p3[0],
            jnp.where(lane8 < 2 * GR, pltpu.roll(p3[1], GR, axis=1),
                      pltpu.roll(p3[2], 2 * GR, axis=1)),
        )
    for k in near:
        start(("pr", k), pq.at[zc(k)], pr.at[z], pr_s.at[k], pr_r.at[NZ - k], dev(zc(k), c, b),
              pr.at[zc(k)], pr_r.at[k])
    landed("h0")
    landed("h1")
    product(1, halo_at)
    send_sum(1, 1, 0)
    send_sum(1, 0, 0)
    if cut(5):
        return

    for k in range(1, NZ):
        landed(("ga", k))
    start("gh", ga, gh, gh_s, gh_r, dev(z, oc, nbr), gh, gh_r)

    inv = gm[:, 0:GR]

    def of_variants(ref):
        gx = jnp.concatenate([ref[j] for j in range(NZ)], axis=1)
        centred = jnp.where(rowg < NC, gx - colmean * gx[GONE:GONE + 1, :], 0.0)
        explained = jnp.sum(centred * mm(inv, centred, HIGH), axis=0, keepdims=True)
        weight = 1.0 / (jnp.maximum(gx[GSP:GSP + 1, :] - explained, 0.0) + EPS)
        return mm(inv, jnp.where((rowg < NC) | (rowg == GONE), gx, 0.0), HIGH), weight

    beta_own, weight_own = of_variants(ga)
    order = ((0, 0), (0, 1), (1, 1), (1, 0))
    for kind, way in order:
        send_sum(kind, way, 1)
    landed("gh")
    beta_halo, weight_halo = of_variants(gh)
    for kind, way in order:
        send_sum(kind, way, 2)

    gene24 = lax.rem(iota((CH, 1), 0), NG)
    first = jnp.zeros((CH, 1), jnp.int32)
    last = jnp.zeros((CH, 1), jnp.int32)
    for g in range(NG):
        first = jnp.where(gene24 == g, win[0, b * NG + g], first)
        last = jnp.where(gene24 == g, win[1, b * NG + g], last)
    base = b * VB - VH + c * VB + iota((CH, VH), 1)

    for k in range(1, NZ):
        landed(("pr", k))
    pr[z] = pq[z]
    tot = pr[0]
    for j in range(1, NZ):
        tot = tot + pr[j]
    proj = jnp.concatenate(
        [tot, pltpu.roll(tot, 128 - GR, axis=1), pltpu.roll(tot, 128 - 2 * GR, axis=1)], axis=0
    )
    l24 = iota((CH, 128), 1)
    proj = jnp.where((l24 < NC) | (l24 == GONE), proj, 0.0)[:, 0:GR]

    for kind, (at, beta_g, weight) in enumerate(
        ((own_at, beta_own, weight_own), (halo_at, beta_halo, weight_halo))
    ):
        lines = pl.ds(pl.multiple_of(z * CH, CH), CH)
        ds[kind, lines, :] = ds[kind, lines, :] - mm(proj, beta_g, HIGH)
        pos = base + at
        wm[kind] = jnp.where((pos >= first) & (pos < last), weight, 0.0)
    for kind, way in order:
        if hops(kind, way) > 3:
            send_sum(kind, way, 3)

    best = jnp.zeros((CH, HW), F32)
    for kind in range(2):
        parts = halves(chunk(kind, 0))
        for way in (0, 1) if hops(kind, 1) > 3 else (1, 0):
            end = hops(kind, way) - 1
            landed(("rs", kind, way, end))
            landed(("sc", kind, way, end))
            got = unpack(rb.at[kind, way, end], sb.at[kind, way, end])
            parts = [u + v for u, v in zip(parts, got)]
        for h in range(2):
            best = jnp.maximum(best, parts[h] * parts[h] * wm[kind, :, HW * h:HW * (h + 1)])
    if cut(6):
        return
    best = jnp.max(best, axis=1, keepdims=True) * float(NSAMP)

    r24, l24 = iota((CH, 128), 0), iota((CH, 128), 1)
    placed = jnp.where(l24 == lax.shift_right_logical(r24, 2) + PZ * z, best, 0.0)
    placed = (placed[0:8] + placed[8:16]) + placed[16:24]
    fm[c, z] = placed + pltpu.roll(placed, NG, axis=0)
    for cc in range(2):
        to = lax.rem(c + cc, 2)
        for k in near + ((0,) if cc else ()):
            start(("o", cc, k), fm.at[c, z], fm.at[c, z], o_s.at[cc, k],
                  o_r.at[cc, (NZ - k) % NZ], dev(zc(k), to, b), fm.at[to, zc(k)], o_r.at[cc, k])
    for key in [("o", 1, 0)] + [("o", cc, k) for k in near for cc in range(2)]:
        landed(key)
    both = [fm[cc, 0] for cc in range(2)]
    for j in range(1, NZ):
        both = [v + fm[cc, j] for cc, v in enumerate(both)]
    peak = jnp.maximum(both[0], both[1])
    columns = peak.T
    level = LEVMAX * iota((NP, 128), 1).astype(F32) / (LEVELS - 1)
    out_ref[0:NG, :] = peak[0:NG]
    for g in range(NG):
        curve = jax.nn.sigmoid(columns[0:NP, g:g + 1] - level)
        out_ref[NG + g:NG + g + 1, :] = jnp.sum(curve, axis=0, keepdims=True) * (1.0 / NP)
    stop()


def split(both_ref, cur_ref, peak_ref):
    peak_ref[...] = both_ref[0:NG, 0:NP]
    cur_ref[...] = both_ref[NG:2 * NG, 0:LEVELS]


def per_device(upto, geno, covar, pheno, perm, windows):
    dma = pltpu.SemaphoreType.DMA
    vmem = pltpu.VMEM
    spec = pl.BlockSpec(memory_space=pltpu.VMEM)
    both = pl.pallas_call(
        functools.partial(kernel, upto),
        out_shape=jax.ShapeDtypeStruct((2 * NG, 128), F32),
        in_specs=[pl.BlockSpec(memory_space=pltpu.HBM)] * 5,
        out_specs=spec,
        scratch_shapes=[
            vmem((NP, NS), jnp.int32),
            pltpu.SMEM((2, NG * NB), jnp.int32),
            vmem((NZ, NC, NS), BF16),
            vmem((NZ, NG, NS), F32),
            vmem((2, XR, NS), BF16),
            vmem((2, NS, VB), BF16),
            vmem((2, GR, 128), F32),
            vmem((NZ, 16, 128), F32),
            vmem((GR, 128), F32),
            vmem((NZ, GR, 128), F32),
            vmem((NZ, GR, 128), F32),
            vmem((NZ, GR, 128), F32),
            vmem((NZ, GR, 128), F32),
            vmem((2, NZ, NG, NS), F32),
            vmem((TR, LO), F32),
            vmem((2, ROWS, NS), BF16),
            vmem((2, ROWS, VH), F32),
            vmem((NZ, 8, 128), F32),
            vmem((NZ, 8, 128), F32),
            vmem((2, 2, 2 * CH, HW), jnp.int16),
            vmem((2, 2, 2, HW), F32),
            vmem((2, 2, 4, 2 * CH, HW), jnp.int16),
            vmem((2, 2, 4, 2, HW), F32),
            vmem((2, CH, VH), F32),
            vmem((2, NZ, 8, 128), F32),
            dma((4,)), dma,
            dma, dma, dma, dma,
            dma((NZ,)), dma((NZ,)),
            dma((2, NZ)), dma((2, NZ)),
            dma, dma,
            dma((2,)), dma((2,)),
            dma((NZ,)), dma((NZ,)),
            dma((NZ,)), dma((NZ,)),
            dma, dma, dma, dma,
            dma((3,)), dma((3,)),
            dma((NZ,)), dma((NZ,)),
            dma((2, 2, 2, 4)), dma((2, 2, 2, 4)),
            dma((2, NZ)), dma((2, NZ)),
        ],
        compiler_params=pltpu.CompilerParams(
            collective_id=0, has_side_effects=True, vmem_limit_bytes=56 * 1024 * 1024
        ),
        name="scan",
    )(geno, covar.T, pheno.T, perm, windows.T)
    return pl.pallas_call(
        split,
        out_shape=(
            jax.ShapeDtypeStruct((NG, LEVELS), F32),
            jax.ShapeDtypeStruct((NG, NP), F32),
        ),
        in_specs=[spec],
        out_specs=(spec, spec),
        name="split",
    )(both)


def build(mesh, upto):
    in_specs = (P("samp", "var"), P("samp", None), P("samp", "var"), P(None, "samp"), P())
    out_specs = (P("var", None), P("var", None))
    return jax.shard_map(
        functools.partial(per_device, upto), mesh=mesh, in_specs=in_specs, out_specs=out_specs,
        check_vma=False,
    )


def solution(mesh):
    return build(mesh, 9)
```

```python
import functools

import jax
import jax.numpy as jnp
from jax import lax
from jax.experimental import pallas as pl
from jax.experimental.pallas import tpu as pltpu
from jax.sharding import PartitionSpec as P

MESH = pl.DeviceIdType.MESH
F32 = jnp.float32
BF16 = jnp.bfloat16
I16 = jnp.int16
HIGH = lax.Precision.HIGHEST

EPS = 1e-06
LEVMAX = 40.0
LEVELS = 64

NZ = 8
NB = 16
NS = 512
NSAMP = 8192
VB = 2048
VH = 1024
NG = 4
NP = 48
NC = 32
XR = 48
ONE = 44
SPARE = 45
GR = 40
GONE = 36
GSP = 37
ROWS = NG * NP
CH = ROWS // NZ
WA = 768
WB = VH - WA
WIDTHS = (VH, WA, WB)
QMAX = 32767.0
TINY = 1e-30
HOPS = (4, 3)
LO = 256
TR = NSAMP // LO * NG
PZ = NP // NZ


def nt(a, b):
    return lax.dot_general(a, b, (((1,), (1,)), ((), ())), preferred_element_type=F32)


def mm(a, b, precision=None):
    return lax.dot_general(
        a, b, (((1,), (0,)), ((), ())), preferred_element_type=F32, precision=precision
    )


def iota(shape, dim):
    return lax.broadcasted_iota(jnp.int32, shape, dim)


def fold_rows(v):
    head, body, tail = v[0:32], v[32:40], v[40:48]
    low = iota(body.shape, 0) < 4
    return jnp.concatenate(
        [head, jnp.where(low, body + pltpu.roll(body, 4, axis=0) + tail, tail)], axis=0
    )


def kernel(
    upto,
    geno, covh, pheh, permh, winh,
    out_ref,
    perm, win, xc, xy, xp, gs, gg, pk, gm, gcp, gr, ga, gh, yt, tab, yo, ds,
    pq, pr, q0, s0, rb, sb, qd, sd, rd, td, wm, fm,
    in_sem, geno_sem, g1_s, g1_r, p_s, p_r, pk_s, pk_r, c_s, c_r, f_s, f_r, h_s, h_r,
    gr_s, gr_r, ga_s, ga_r, gh_s, gh_r, t_s, t_r, y_s, y_r,
    pr_s, pr_r, rs_s, rs_r, d_s, d_r, o_s, o_r,
):
    s = lax.axis_index("samp")
    b = lax.axis_index("var")
    z = lax.div(s, 2)
    c = lax.rem(s, 2)
    oc = 1 - c
    up_band = lax.rem(b + 1, NB)
    down_band = lax.rem(b + NB - 1, NB)
    nbr = lax.rem(b + 2 * c - 1 + NB, NB)
    own_at = pl.multiple_of(oc * VH, VH)
    halo_at = pl.multiple_of(c * VH, VH)

    def zc(k):
        return lax.rem(z + k % NZ, NZ)

    def dev(zz, cc, bb):
        return {"samp": zz * 2 + cc, "var": bb}

    def half(cc):
        return pl.ds(pl.multiple_of(cc * VH, VH), VH)

    sent, due = [], {}

    def start(key, src, dst, ss, rs, to, here, here_sem):
        d = pltpu.make_async_remote_copy(
            src_ref=src, dst_ref=dst, send_sem=ss, recv_sem=rs, device_id=to, device_id_type=MESH
        )
        d.start()
        sent.append(d)
        due[key] = (here, here_sem)

    def landed(key):
        here, sem = due.pop(key)
        pltpu.make_async_remote_copy(
            src_ref=here, dst_ref=here, send_sem=sem, recv_sem=sem,
            device_id=dev(z, oc, b), device_id_type=MESH,
        ).wait_recv()

    def stop():
        for key in list(due):
            landed(key)
        for d in sent:
            d.wait_send()

    def cut(level):
        if upto != level:
            return False
        stop()
        out_ref[...] = jnp.zeros_like(out_ref)
        return True

    other = dev(z, oc, b)
    loads = [
        pltpu.make_async_copy(src, dst, in_sem.at[i])
        for i, (src, dst) in enumerate((
            (covh, xc.at[z]), (pheh, xy.at[z]), (permh, perm), (winh, win),
        ))
    ]
    for d in loads:
        d.start()
    barrier = pltpu.get_barrier_semaphore()
    peers = [dev(zc(k), cc, b) for k in range(1, NZ) for cc in (0, 1)] + [other]
    peers += [dev(z, cc, bb) for cc in (0, 1) for bb in (up_band, down_band)]
    for peer in peers:
        pl.semaphore_signal(barrier, inc=1, device_id=peer, device_id_type=MESH)
    own_geno = pltpu.make_async_copy(geno.at[:, half(c)], gs.at[c, :, pl.ds(own_at, VH)], geno_sem)
    own_geno.start()
    for d in loads:
        d.wait()

    phe = xy[z]
    full = jnp.concatenate([phe, phe], axis=0)
    hi = full.astype(BF16).astype(F32)
    rest = full - hi
    mid = rest.astype(BF16).astype(F32)
    low = (rest - mid).astype(BF16).astype(F32)
    row8 = iota((8, NS), 0)
    block_a = jnp.where(row8 < 4, hi, mid)
    block_b = jnp.where(row8 < 4, low, jnp.where(row8 == 4, 1.0, 0.0))
    xp[c] = jnp.concatenate([xc[z].astype(F32), block_a, block_b], axis=0).astype(BF16)
    mine = xp[c]
    gg[c] = jnp.zeros((GR, 128), F32)
    gg[c, :, 0:XR] = fold_rows(nt(mine, mine))

    pl.semaphore_wait(barrier, len(peers))
    start("g1", gg.at[c], gg.at[c], g1_s, g1_r, other, gg.at[oc], g1_r)
    start("p", xp.at[c], xp.at[c], p_s, p_r, other, xp.at[oc], p_r)

    def send_halo(piece):
        skip, width = ((0, WA), (WA, WB))[piece]
        for i, (cc, band) in enumerate(((0, up_band), (1, down_band))):
            start(
                ("h", piece, i), geno.at[:, pl.ds((1 - cc) * VH + skip, width)],
                gs.at[c, :, pl.ds(cc * VH + skip, width)], h_s.at[piece, i], h_r.at[piece, c],
                dev(z, cc, band),
                gs.at[i, :, pl.ds(pl.multiple_of(halo_at + skip, 128), width)], h_r.at[piece, i],
            )

    send_halo(0)
    if cut(0):
        own_geno.wait()
        return

    landed("g1")
    g = gg[0] + gg[1]
    lane40 = iota((GR, 128), 1)
    g = jnp.where(lane40 < GONE, g, pltpu.roll(g, 128 - (ONE - GONE), axis=1))
    g = jnp.concatenate([g, jnp.zeros((8, 128), F32)], axis=0)
    lane16 = iota((16, 128), 1)
    pk[z] = jnp.where(
        lane16 < GR, g[0:16],
        jnp.where(lane16 < 2 * GR, pltpu.roll(g[16:32], GR, axis=1),
                  jnp.where(lane16 < 3 * GR, pltpu.roll(g[32:48], 2 * GR, axis=1), 0.0)),
    )
    near = (1, 7, 2, 6, 3, 5, 4)
    for k in near:
        start(("pk", k), pk.at[z], pk.at[z], pk_s.at[k], pk_r.at[NZ - k], dev(zc(k), c, b),
              pk.at[zc(k)], pk_r.at[k])
    start("f", geno.at[:, half(oc)], gs.at[c, :, half(c)], f_s, f_r, other,
          gs.at[oc, :, pl.ds(own_at, VH)], f_r)

    def share(name, held, to):
        ref = (xc, xy)[name == "y"]
        i, k, got = int(name == "y"), (held - to) % NZ, zc(held - to)
        start((name, k), ref.at[zc(held)], ref.at[zc(held)], c_s.at[i, k], c_r.at[i, k],
              dev(zc(to), c, b), ref.at[got], c_r.at[i, k])

    for to in (1, -1, 2, -2):
        share("c", 0, to)
        share("y", 0, to)
    own_geno.wait()
    landed("f")
    landed("p")
    gpart = fold_rows(
        mm(xp[0], gs[0, :, pl.ds(own_at, VH)]) + mm(xp[1], gs[1, :, pl.ds(own_at, VH)])
    )
    for name in ("c", "y"):
        for k in (6, 2):
            landed((name, k))
    share("c", -2, 2)
    share("y", 2, -2)
    for name in ("c", "y"):
        share(name, -2, 1)
        share(name, 2, -1)
    mean = gpart[GONE:GONE + 1, :] * (1.0 / (2 * NS))

    def spread(i, acc):
        at = pl.ds(pl.multiple_of(lax.rem(i, 32) * 16, 16), 16)
        dif = gs[lax.div(i, 32), at, pl.ds(own_at, VH)].astype(F32) - mean
        return acc + dif * dif

    acc = lax.fori_loop(0, 64, spread, jnp.zeros((16, VH), F32), unroll=4)
    rowg = iota((GR, VH), 0)
    gpart = jnp.where(rowg == GSP, jnp.sum(acc, axis=0, keepdims=True), gpart)
    for j in range(NZ):
        gcp[j] = gpart[:, j * 128:(j + 1) * 128]
    for k in near:
        start(("gr", k), gcp.at[zc(k)], gr.at[z], gr_s.at[k], gr_r.at[NZ - k], dev(zc(k), c, b),
              gr.at[zc(k)], gr_r.at[k])

    for k in range(1, NZ):
        landed(("pk", k))
    if cut(1):
        return
    tot = pk[0]
    for j in range(1, NZ):
        tot = tot + pk[j]
    a = jnp.concatenate(
        [tot, pltpu.roll(tot, 128 - GR, axis=1), pltpu.roll(tot, 128 - 2 * GR, axis=1)[0:8]], axis=0
    )
    row, lane = iota((GR, 128), 0), iota((GR, 128), 1)
    in_row = (row < NC) | (row == GONE)
    in_lane = (lane < NC) | (lane == GONE)
    a = jnp.where(in_lane, a, 0.0)
    colmean = a[:, GONE:GONE + 1] * (1.0 / NSAMP)
    for k in (GONE,) + tuple(range(NC)):
        q = a[:, k:k + 1]
        r = a[k:k + 1, :]
        inv = 1.0 / a[k:k + 1, k:k + 1]
        rr = r * inv
        nxt = a - q * rr
        nxt = jnp.where(row == k, rr, nxt)
        nxt = jnp.where(lane == k, jnp.where(row == k, -inv, q * inv), nxt)
        a = nxt
    gm[...] = jnp.where(in_row & in_lane, -a, 0.0)

    beta = a[32:40, :]
    row24 = beta.astype(BF16).astype(F32)
    rest = beta - row24
    mid = rest.astype(BF16).astype(F32)
    coefs = jnp.concatenate([row24, mid, rest - mid], axis=0)[:, 0:NC].astype(BF16)
    const = beta[0:4, GONE:GONE + 1]
    if cut(2):
        return
    for k in (0, 7, 1, 6, 2, 5, 3, 4):
        for name in ("c", "y"):
            if (name, k) in due:
                landed((name, k))
        t = mm(coefs, xc[zc(k)])
        fit = (t[16:24] + t[8:16]) + t[0:8]
        yt[c, zc(k)] = xy[zc(k)] - (fit[0:4] + const)
    start("t", yt.at[c], yt.at[c], t_s, t_r, other, yt.at[oc], t_r)
    send_halo(1)

    landed("t")
    ysq = jnp.zeros((NG, NS), F32)
    for cc in range(2):
        for j in range(NZ):
            ysq = ysq + yt[cc, j] * yt[cc, j]
    ynorm = jnp.sqrt(jnp.sum(ysq, axis=1, keepdims=True) + EPS)
    for cc in range(2):
        for j in range(NZ):
            y = yt[cc, j] / ynorm
            for q in range(2):
                at = (2 * (2 * j + cc) + q) * NG
                tab[at:at + NG, :] = y[:, q * LO:(q + 1) * LO]
    if cut(3):
        return

    table = tab[...].astype(BF16)
    count = iota((LO, NS), 0).astype(F32).astype(BF16)
    holds = lax.shift_right_logical(iota((TR, NS), 0), 2)
    low_half = iota((8, NS), 0) < NG
    one = jnp.ones((), BF16)
    zero = jnp.zeros((), BF16)

    def look(i, carry):
        got = []
        for u in range(4):
            idx = perm[pl.ds(i * 4 + u, 1), :]
            ilo = lax.bitwise_and(idx, LO - 1).astype(F32).astype(BF16)
            found = mm(table, jnp.where(count == ilo, one, zero))
            found = jnp.where(holds == lax.shift_right_logical(idx, 8), found, 0.0)
            part = found[0:8]
            for j in range(1, TR // 8):
                part = part + found[j * 8:(j + 1) * 8]
            got.append(part + pltpu.roll(part, NG, axis=0))
        rows = jnp.concatenate(
            [jnp.where(low_half, got[0], got[1]), jnp.where(low_half, got[2], got[3])], axis=0
        )
        yo[c, pl.ds(pl.multiple_of(i * 16, 16), 16), :] = rows.astype(BF16)
        return carry

    def sum_variants():
        for k in range(1, NZ):
            landed(("gr", k))
        gr[z] = gcp[z]
        tot = gr[0]
        for j in range(1, NZ):
            tot = tot + gr[j]
        mu = tot[GONE:GONE + 1, :] * (1.0 / NSAMP)
        between = jnp.zeros((1, 128), F32)
        for j in range(NZ):
            off = gr[j, GONE:GONE + 1, :] * (1.0 / (2 * NS)) - mu
            between = between + off * off
        ga[z] = tot + jnp.where(row == GSP, between * (2.0 * NS), 0.0)
        for k in near:
            start(("ga", k), ga.at[z], ga.at[z], ga_s.at[k], ga_r.at[NZ - k], dev(zc(k), c, b),
                  ga.at[zc(k)], ga_r.at[k])

    for j in range(3):
        lax.fori_loop(j * 4, j * 4 + 4, look, 0)
        part = pl.ds(j * 64, 64)
        start(("yo", j), yo.at[c, part], yo.at[c, part], y_s.at[j], y_r.at[j], other,
              yo.at[oc, part], y_r.at[j])
        if j == 0:
            sum_variants()
    if cut(4):
        return
    for j in range(3):
        landed(("yo", j))

    def product(kind, at):
        lanes = pl.ds(pl.multiple_of(at, 128), WIDTHS[kind])
        ds[kind][...] = mm(yo[0], gs[0, :, lanes]) + mm(yo[1], gs[1, :, lanes])

    def chunk(kind, k):
        return ds[kind].at[pl.ds(pl.multiple_of(zc(k) * CH, CH), CH)]

    def hops(kind, way):
        return HOPS[(kind + way) % 2]

    def unpack(ref, scale):
        q = ref[...].astype(F32)
        return [q[CH * h:CH * (h + 1)] * scale[h:h + 1, :] for h in range(2)]

    def halves(ref):
        w = ref.shape[1] // 2
        return [ref[:, w * h:w * (h + 1)] for h in range(2)]

    def pack(parts, ref, scale):
        codes = []
        for h in range(2):
            top = jnp.max(jnp.abs(parts[h]), axis=0, keepdims=True)
            top = jnp.maximum(top, TINY)
            scale[h:h + 1, :] = top * (1.0 / QMAX)
            codes.append(jnp.round(parts[h] * (QMAX / top)))
        ref[...] = jnp.concatenate(codes, axis=0).astype(jnp.int32).astype(jnp.int16)

    def send_sum(kind, way, t):
        n = hops(kind, way)
        sign = 1 - 2 * way
        parts = halves(chunk(kind, -sign * (n - t)))
        if t == 0:
            src, scale = q0[kind].at[way], s0[kind].at[way]
        else:
            src, scale = rb[kind].at[way, t - 1], sb[kind].at[way, t - 1]
            landed(("rs", kind, way, t - 1))
            landed(("sc", kind, way, t - 1))
            parts = [u + v for u, v in zip(parts, unpack(src, scale))]
        pack(parts, src, scale)
        to = dev(zc(-sign), c, b)
        for i, (name, here, buf) in enumerate((("rs", src, rb), ("sc", scale, sb))):
            land = buf[kind].at[way, t]
            start((name, kind, way, t), here, land, rs_s.at[i, kind, way, t],
                  rs_r.at[i, kind, way, t], to, land, rs_r.at[i, kind, way, t])

    product(0, own_at)
    send_sum(0, 0, 0)
    send_sum(0, 1, 0)

    proj = jnp.concatenate(
        [nt(yo[0], xp[0]) + nt(yo[1], xp[1]), jnp.zeros((ROWS, 128 - XR), F32)], axis=1
    )
    proj = jnp.where(iota((ROWS, 128), 1) < GONE, proj, pltpu.roll(proj, 128 - (ONE - GONE), axis=1))
    lane8 = iota((8, 128), 1)
    for j in range(NZ):
        p3 = [proj[CH * j + 8 * i:CH * j + 8 * i + 8] for i in range(3)]
        pq[j] = jnp.where(
            lane8 < GR, p3[0],
            jnp.where(lane8 < 2 * GR, pltpu.roll(p3[1], GR, axis=1),
                      pltpu.roll(p3[2], 2 * GR, axis=1)),
        )
    for k in near:
        start(("pr", k), pq.at[zc(k)], pr.at[z], pr_s.at[k], pr_r.at[NZ - k], dev(zc(k), c, b),
              pr.at[zc(k)], pr_r.at[k])
    landed(("h", 0, 0))
    landed(("h", 0, 1))
    product(1, halo_at)
    send_sum(1, 1, 0)
    send_sum(1, 0, 0)
    if cut(5):
        return

    for k in range(1, NZ):
        landed(("ga", k))
    start("gh", ga, gh, gh_s, gh_r, dev(z, oc, nbr), gh, gh_r)

    inv = gm[:, 0:GR]

    def of_variants(ref):
        gx = jnp.concatenate([ref[j] for j in range(NZ)], axis=1)
        centred = jnp.where(rowg < NC, gx - colmean * gx[GONE:GONE + 1, :], 0.0)
        explained = jnp.sum(centred * mm(inv, centred, HIGH), axis=0, keepdims=True)
        weight = 1.0 / (jnp.maximum(gx[GSP:GSP + 1, :] - explained, 0.0) + EPS)
        return mm(inv, jnp.where((rowg < NC) | (rowg == GONE), gx, 0.0), HIGH), weight

    beta_own, weight_own = of_variants(ga)
    order = ((0, 0), (0, 1), (1, 1), (1, 0))
    for kind, way in order:
        send_sum(kind, way, 1)

    landed(("h", 1, 0))
    landed(("h", 1, 1))
    product(2, halo_at + WA)
    for k in near:
        pack(halves(chunk(2, k)), qd.at[zc(k)], sd.at[zc(k)])
        for i, (name, here, there) in enumerate((("dr", qd, rd), ("dc", sd, td))):
            start((name, k), here.at[zc(k)], there.at[z], d_s.at[i, k], d_r.at[i, NZ - k],
                  dev(zc(k), c, b), there.at[zc(k)], d_r.at[i, k])
    landed("gh")
    beta_halo, weight_halo = of_variants(gh)
    for kind, way in order:
        send_sum(kind, way, 2)

    gene24 = lax.rem(iota((CH, 1), 0), NG)
    first = jnp.zeros((CH, 1), jnp.int32)
    last = jnp.zeros((CH, 1), jnp.int32)
    for g in range(NG):
        first = jnp.where(gene24 == g, win[0, b * NG + g], first)
        last = jnp.where(gene24 == g, win[1, b * NG + g], last)
    base = b * VB - VH + c * VB + iota((CH, VH), 1)

    for k in range(1, NZ):
        landed(("pr", k))
    pr[z] = pq[z]
    tot = pr[0]
    for j in range(1, NZ):
        tot = tot + pr[j]
    proj = jnp.concatenate(
        [tot, pltpu.roll(tot, 128 - GR, axis=1), pltpu.roll(tot, 128 - 2 * GR, axis=1)], axis=0
    )
    l24 = iota((CH, 128), 1)
    proj = jnp.where((l24 < NC) | (l24 == GONE), proj, 0.0)[:, 0:GR]

    fits = (
        (own_at, beta_own, weight_own),
        (halo_at, beta_halo[:, 0:WA], weight_halo[:, 0:WA]),
        (halo_at + WA, beta_halo[:, WA:VH], weight_halo[:, WA:VH]),
    )
    lines = pl.ds(pl.multiple_of(z * CH, CH), CH)
    for kind, (at, beta_g, weight) in enumerate(fits):
        ds[kind][lines, :] = ds[kind][lines, :] - mm(proj, beta_g, HIGH)
        pos = base[:, 0:WIDTHS[kind]] + at
        wm[kind][...] = jnp.where((pos >= first) & (pos < last), weight, 0.0)
    for kind, way in order:
        if hops(kind, way) > 3:
            send_sum(kind, way, 3)

    def squares(kind, parts):
        v = jnp.concatenate(parts, axis=1)
        v = v * v * wm[kind][...]
        return functools.reduce(
            jnp.maximum, [v[:, i:i + 128] for i in range(0, WIDTHS[kind], 128)]
        )

    parts = halves(chunk(2, 0))
    for k in near:
        landed(("dr", k))
        landed(("dc", k))
        parts = [u + v for u, v in zip(parts, unpack(rd.at[zc(k)], td.at[zc(k)]))]
    best = squares(2, parts)
    for kind in range(2):
        parts = halves(chunk(kind, 0))
        for way in (0, 1) if hops(kind, 1) > 3 else (1, 0):
            end = hops(kind, way) - 1
            landed(("rs", kind, way, end))
            landed(("sc", kind, way, end))
            got = unpack(rb[kind].at[way, end], sb[kind].at[way, end])
            parts = [u + v for u, v in zip(parts, got)]
        best = jnp.maximum(best, squares(kind, parts))
    if cut(6):
        return
    best = jnp.max(best, axis=1, keepdims=True) * float(NSAMP)

    r24, l24 = iota((CH, 128), 0), iota((CH, 128), 1)
    placed = jnp.where(l24 == lax.shift_right_logical(r24, 2) + PZ * z, best, 0.0)
    placed = (placed[0:8] + placed[8:16]) + placed[16:24]
    fm[c, z] = (placed + pltpu.roll(placed, NG, axis=0))[0:NG]
    for cc in range(2):
        to = lax.rem(c + cc, 2)
        for k in near + ((0,) if cc else ()):
            start(("o", cc, k), fm.at[c, z], fm.at[c, z], o_s.at[cc, k],
                  o_r.at[cc, (NZ - k) % NZ], dev(zc(k), to, b), fm.at[to, zc(k)], o_r.at[cc, k])
    for key in [("o", 1, 0)] + [("o", cc, k) for k in near for cc in range(2)]:
        landed(key)
    both = [fm[cc, 0] for cc in range(2)]
    for j in range(1, NZ):
        both = [v + fm[cc, j] for cc, v in enumerate(both)]
    peak = jnp.maximum(both[0], both[1])
    columns = jnp.concatenate([peak, peak], axis=0).T
    level = LEVMAX * iota((NP, 128), 1).astype(F32) / (LEVELS - 1)
    out_ref[0:NG, :] = peak
    for g in range(NG):
        curve = jax.nn.sigmoid(columns[0:NP, g:g + 1] - level)
        out_ref[NG + g:NG + g + 1, :] = jnp.sum(curve, axis=0, keepdims=True) * (1.0 / NP)
    stop()


def split(both_ref, cur_ref, peak_ref):
    peak_ref[...] = both_ref[0:NG, 0:NP]
    cur_ref[...] = both_ref[NG:2 * NG, 0:LEVELS]


def per_device(upto, geno, covar, pheno, perm, windows):
    dma = pltpu.SemaphoreType.DMA
    vmem = pltpu.VMEM
    spec = pl.BlockSpec(memory_space=pltpu.VMEM)
    both = pl.pallas_call(
        functools.partial(kernel, upto),
        out_shape=jax.ShapeDtypeStruct((2 * NG, 128), F32),
        in_specs=[pl.BlockSpec(memory_space=pltpu.HBM)] * 5,
        out_specs=spec,
        scratch_shapes=[
            vmem((NP, NS), jnp.int32),
            pltpu.SMEM((2, NG * NB), jnp.int32),
            vmem((NZ, NC, NS), BF16),
            vmem((NZ, NG, NS), F32),
            vmem((2, XR, NS), BF16),
            vmem((2, NS, VB), BF16),
            vmem((2, GR, 128), F32),
            vmem((NZ, 16, 128), F32),
            vmem((GR, 128), F32),
            vmem((NZ, GR, 128), F32),
            vmem((NZ, GR, 128), F32),
            vmem((NZ, GR, 128), F32),
            vmem((NZ, GR, 128), F32),
            vmem((2, NZ, NG, NS), F32),
            vmem((TR, LO), F32),
            vmem((2, ROWS, NS), BF16),
            [vmem((ROWS, w), F32) for w in WIDTHS],
            vmem((NZ, 8, 128), F32),
            vmem((NZ, 8, 128), F32),
            [vmem((2, 2 * CH, w // 2), I16) for w in WIDTHS[:2]],
            [vmem((2, 2, w // 2), F32) for w in WIDTHS[:2]],
            [vmem((2, 4, 2 * CH, w // 2), I16) for w in WIDTHS[:2]],
            [vmem((2, 4, 2, w // 2), F32) for w in WIDTHS[:2]],
            vmem((NZ, 2 * CH, WB // 2), I16),
            vmem((NZ, 2, WB // 2), F32),
            vmem((NZ, 2 * CH, WB // 2), I16),
            vmem((NZ, 2, WB // 2), F32),
            [vmem((CH, w), F32) for w in WIDTHS],
            vmem((2, NZ, NG, 128), F32),
            dma((4,)), dma,
            dma, dma, dma, dma,
            dma((NZ,)), dma((NZ,)),
            dma((2, NZ)), dma((2, NZ)),
            dma, dma,
            dma((2, 2)), dma((2, 2)),
            dma((NZ,)), dma((NZ,)),
            dma((NZ,)), dma((NZ,)),
            dma, dma, dma, dma,
            dma((3,)), dma((3,)),
            dma((NZ,)), dma((NZ,)),
            dma((2, 2, 2, 4)), dma((2, 2, 2, 4)),
            dma((2, NZ)), dma((2, NZ)),
            dma((2, NZ)), dma((2, NZ)),
        ],
        compiler_params=pltpu.CompilerParams(
            collective_id=0, has_side_effects=True, vmem_limit_bytes=56 * 1024 * 1024
        ),
        name="scan",
    )(geno, covar.T, pheno.T, perm, windows.T)
    return pl.pallas_call(
        split,
        out_shape=(
            jax.ShapeDtypeStruct((NG, LEVELS), F32),
            jax.ShapeDtypeStruct((NG, NP), F32),
        ),
        in_specs=[spec],
        out_specs=(spec, spec),
        name="split",
    )(both)


def build(mesh, upto):
    in_specs = (P("samp", "var"), P("samp", None), P("samp", "var"), P(None, "samp"), P())
    out_specs = (P("var", None), P("var", None))
    return jax.shard_map(
        functools.partial(per_device, upto), mesh=mesh, in_specs=in_specs, out_specs=out_specs,
        check_vma=False,
    )


def solution(mesh):
    return build(mesh, 9)
```

```python
import functools

import jax
import jax.numpy as jnp
from jax import lax
from jax.experimental import pallas as pl
from jax.experimental.pallas import tpu as pltpu
from jax.sharding import PartitionSpec as P

MESH = pl.DeviceIdType.MESH
F32 = jnp.float32
BF16 = jnp.bfloat16
I16 = jnp.int16
HIGH = lax.Precision.HIGHEST

EPS = 1e-06
LEVMAX = 40.0
LEVELS = 64

NZ = 8
NB = 16
NS = 512
NSAMP = 8192
VB = 2048
VH = 1024
NG = 4
NP = 48
NC = 32
XR = 48
ONE = 44
SPARE = 45
GR = 40
GONE = 36
GSP = 37
ROWS = NG * NP
CH = ROWS // NZ
WA = 768
WB = VH - WA
WIDTHS = (VH, WA, WB)
QMAX = 32767.0
TINY = 1e-30
HOPS = (4, 3)
LO = 256
TR = NSAMP // LO * NG
PZ = NP // NZ


def nt(a, b):
    return lax.dot_general(a, b, (((1,), (1,)), ((), ())), preferred_element_type=F32)


def mm(a, b, precision=None):
    return lax.dot_general(
        a, b, (((1,), (0,)), ((), ())), preferred_element_type=F32, precision=precision
    )


def iota(shape, dim):
    return lax.broadcasted_iota(jnp.int32, shape, dim)


def fold_rows(v):
    head, body, tail = v[0:32], v[32:40], v[40:48]
    low = iota(body.shape, 0) < 4
    return jnp.concatenate(
        [head, jnp.where(low, body + pltpu.roll(body, 4, axis=0) + tail, tail)], axis=0
    )


def kernel(
    upto,
    geno, covh, pheh, permh, winh,
    out_ref,
    perm, win, xc, xy, xp, gs, gg, pk, gm, gcp, gr, ga, gh, yt, tab, yo, ds,
    pq, pr, q0, s0, rb, sb, qd, sd, rd, td, wm, fm,
    in_sem, geno_sem, g1_s, g1_r, p_s, p_r, pk_s, pk_r, c_s, c_r, f_s, f_r, h_s, h_r,
    gr_s, gr_r, ga_s, ga_r, gh_s, gh_r, t_s, t_r, y_s, y_r,
    pr_s, pr_r, rs_s, rs_r, d_s, d_r, o_s, o_r,
):
    s = lax.axis_index("samp")
    b = lax.axis_index("var")
    z = lax.div(s, 2)
    c = lax.rem(s, 2)
    oc = 1 - c
    up_band = lax.rem(b + 1, NB)
    down_band = lax.rem(b + NB - 1, NB)
    nbr = lax.rem(b + 2 * c - 1 + NB, NB)
    own_at = pl.multiple_of(oc * VH, VH)
    halo_at = pl.multiple_of(c * VH, VH)

    def zc(k):
        return lax.rem(z + k % NZ, NZ)

    def dev(zz, cc, bb):
        return {"samp": zz * 2 + cc, "var": bb}

    def half(cc):
        return pl.ds(pl.multiple_of(cc * VH, VH), VH)

    sent, due = [], {}

    def start(key, src, dst, ss, rs, to, here, here_sem):
        d = pltpu.make_async_remote_copy(
            src_ref=src, dst_ref=dst, send_sem=ss, recv_sem=rs, device_id=to, device_id_type=MESH
        )
        d.start()
        sent.append(d)
        due[key] = (here, here_sem)

    def landed(key):
        here, sem = due.pop(key)
        pltpu.make_async_remote_copy(
            src_ref=here, dst_ref=here, send_sem=sem, recv_sem=sem,
            device_id=dev(z, oc, b), device_id_type=MESH,
        ).wait_recv()

    def stop():
        for key in list(due):
            landed(key)
        for d in sent:
            d.wait_send()

    def cut(level):
        if upto != level:
            return False
        stop()
        out_ref[...] = jnp.zeros_like(out_ref)
        return True

    other = dev(z, oc, b)
    loads = [
        pltpu.make_async_copy(src, dst, in_sem.at[i])
        for i, (src, dst) in enumerate((
            (covh, xc.at[z]), (pheh, xy.at[z]), (permh, perm), (winh, win),
        ))
    ]
    for d in loads:
        d.start()
    barrier = pltpu.get_barrier_semaphore()
    peers = [dev(zc(k), cc, b) for k in range(1, NZ) for cc in (0, 1)] + [other]
    peers += [dev(z, cc, bb) for cc in (0, 1) for bb in (up_band, down_band)]
    for peer in peers:
        pl.semaphore_signal(barrier, inc=1, device_id=peer, device_id_type=MESH)
    own_geno = pltpu.make_async_copy(geno.at[:, half(c)], gs.at[c, :, pl.ds(own_at, VH)], geno_sem)
    own_geno.start()
    for d in loads:
        d.wait()

    phe = xy[z]
    full = jnp.concatenate([phe, phe], axis=0)
    hi = full.astype(BF16).astype(F32)
    rest = full - hi
    mid = rest.astype(BF16).astype(F32)
    low = (rest - mid).astype(BF16).astype(F32)
    row8 = iota((8, NS), 0)
    block_a = jnp.where(row8 < 4, hi, mid)
    block_b = jnp.where(row8 < 4, low, jnp.where(row8 == 4, 1.0, 0.0))
    xp[c] = jnp.concatenate([xc[z].astype(F32), block_a, block_b], axis=0).astype(BF16)
    mine = xp[c]
    gg[c] = jnp.zeros((GR, 128), F32)
    gg[c, :, 0:XR] = fold_rows(nt(mine, mine))

    pl.semaphore_wait(barrier, len(peers))
    start("g1", gg.at[c], gg.at[c], g1_s, g1_r, other, gg.at[oc], g1_r)
    def send_halo(piece):
        skip, width = ((0, WA), (WA, WB))[piece]
        for i, (cc, band) in enumerate(((0, up_band), (1, down_band))):
            start(
                ("h", piece, i), geno.at[:, pl.ds((1 - cc) * VH + skip, width)],
                gs.at[c, :, pl.ds(cc * VH + skip, width)], h_s.at[piece, i], h_r.at[piece, c],
                dev(z, cc, band),
                gs.at[i, :, pl.ds(pl.multiple_of(halo_at + skip, 128), width)], h_r.at[piece, i],
            )
    send_halo(0)

    def share(name, held, to):
        ref = (xc, xy)[name == "y"]
        i, k, got = int(name == "y"), (held - to) % NZ, zc(held - to)
        start((name, k), ref.at[zc(held)], ref.at[zc(held)], c_s.at[i, k], c_r.at[i, k],
              dev(zc(to), c, b), ref.at[got], c_r.at[i, k])

    for to in (1, -1, 2, -2):
        share("c", 0, to)
        share("y", 0, to)
    start("p", xp.at[c], xp.at[c], p_s, p_r, other, xp.at[oc], p_r)
    if cut(0):
        own_geno.wait()
        return

    landed("g1")
    g = gg[0] + gg[1]
    lane40 = iota((GR, 128), 1)
    g = jnp.where(lane40 < GONE, g, pltpu.roll(g, 128 - (ONE - GONE), axis=1))
    g = jnp.concatenate([g, jnp.zeros((8, 128), F32)], axis=0)
    lane16 = iota((16, 128), 1)
    pk[z] = jnp.where(
        lane16 < GR, g[0:16],
        jnp.where(lane16 < 2 * GR, pltpu.roll(g[16:32], GR, axis=1),
                  jnp.where(lane16 < 3 * GR, pltpu.roll(g[32:48], 2 * GR, axis=1), 0.0)),
    )
    near = (1, 7, 2, 6, 3, 5, 4)
    for k in near:
        start(("pk", k), pk.at[z], pk.at[z], pk_s.at[k], pk_r.at[NZ - k], dev(zc(k), c, b),
              pk.at[zc(k)], pk_r.at[k])
    start("f", geno.at[:, half(oc)], gs.at[c, :, half(c)], f_s, f_r, other,
          gs.at[oc, :, pl.ds(own_at, VH)], f_r)

    for name in ("c", "y"):
        for k in (6, 2):
            landed((name, k))
    share("c", -2, 2)
    share("y", 2, -2)
    for name in ("c", "y"):
        share(name, -2, 1)
        share(name, 2, -1)

    own_geno.wait()
    landed("f")
    landed("p")
    gpart = fold_rows(
        mm(xp[0], gs[0, :, pl.ds(own_at, VH)]) + mm(xp[1], gs[1, :, pl.ds(own_at, VH)])
    )
    mean = gpart[GONE:GONE + 1, :] * (1.0 / (2 * NS))

    def spread(i, acc):
        at = pl.ds(pl.multiple_of(lax.rem(i, 32) * 16, 16), 16)
        dif = gs[lax.div(i, 32), at, pl.ds(own_at, VH)].astype(F32) - mean
        return acc + dif * dif

    acc = lax.fori_loop(0, 64, spread, jnp.zeros((16, VH), F32), unroll=4)
    rowg = iota((GR, VH), 0)
    gpart = jnp.where(rowg == GSP, jnp.sum(acc, axis=0, keepdims=True), gpart)
    for j in range(NZ):
        gcp[j] = gpart[:, j * 128:(j + 1) * 128]
    for k in near:
        start(("gr", k), gcp.at[zc(k)], gr.at[z], gr_s.at[k], gr_r.at[NZ - k], dev(zc(k), c, b),
              gr.at[zc(k)], gr_r.at[k])

    for k in range(1, NZ):
        landed(("pk", k))
    if cut(1):
        return
    tot = pk[0]
    for j in range(1, NZ):
        tot = tot + pk[j]
    a = jnp.concatenate(
        [tot, pltpu.roll(tot, 128 - GR, axis=1), pltpu.roll(tot, 128 - 2 * GR, axis=1)[0:8]], axis=0
    )
    row, lane = iota((GR, 128), 0), iota((GR, 128), 1)
    in_row = (row < NC) | (row == GONE)
    in_lane = (lane < NC) | (lane == GONE)
    a = jnp.where(in_lane, a, 0.0)
    colmean = a[:, GONE:GONE + 1] * (1.0 / NSAMP)
    r = a[GONE:GONE + 1, :]
    inv = 1.0 / a[GONE:GONE + 1, GONE:GONE + 1]
    q = a[:, GONE:GONE + 1]
    nxt = jnp.where(row == GONE, r * inv, a - q * (r * inv))
    a = jnp.where(lane == GONE, jnp.where(row == GONE, -inv, q * inv), nxt)
    for k in range(0, NC, 2):
        m = k + 1
        q1, q2 = a[:, k:k + 1], a[:, m:m + 1]
        r1, r2 = a[k:k + 1, :], a[m:m + 1, :]
        p, o, w = a[k:k + 1, k:k + 1], a[k:k + 1, m:m + 1], a[m:m + 1, m:m + 1]
        det = 1.0 / (p * w - o * o)
        p, o, w = p * det, o * det, w * det
        t1, t2 = w * r1 - o * r2, p * r2 - o * r1
        nxt = a - q1 * t1 - q2 * t2
        nxt = jnp.where(row == k, t1, jnp.where(row == m, t2, nxt))
        c1 = jnp.where(row == k, -w, jnp.where(row == m, o, w * q1 - o * q2))
        c2 = jnp.where(row == k, o, jnp.where(row == m, -p, p * q2 - o * q1))
        a = jnp.where(lane == k, c1, jnp.where(lane == m, c2, nxt))
    gm[...] = jnp.where(in_row & in_lane, -a, 0.0)

    beta = a[32:40, :]
    row24 = beta.astype(BF16).astype(F32)
    rest = beta - row24
    mid = rest.astype(BF16).astype(F32)
    coefs = jnp.concatenate([row24, mid, rest - mid], axis=0)[:, 0:NC].astype(BF16)
    const = beta[0:4, GONE:GONE + 1]
    if cut(2):
        return
    for k in (0, 7, 1, 6, 2, 5, 3, 4):
        for name in ("c", "y"):
            if (name, k) in due:
                landed((name, k))
        t = mm(coefs, xc[zc(k)])
        fit = (t[16:24] + t[8:16]) + t[0:8]
        yt[c, zc(k)] = xy[zc(k)] - (fit[0:4] + const)
    start("t", yt.at[c], yt.at[c], t_s, t_r, other, yt.at[oc], t_r)

    landed("t")
    ysq = jnp.zeros((NG, NS), F32)
    for cc in range(2):
        for j in range(NZ):
            ysq = ysq + yt[cc, j] * yt[cc, j]
    ynorm = jnp.sqrt(jnp.sum(ysq, axis=1, keepdims=True) + EPS)
    for cc in range(2):
        for j in range(NZ):
            y = yt[cc, j] / ynorm
            for q in range(2):
                at = (2 * (2 * j + cc) + q) * NG
                tab[at:at + NG, :] = y[:, q * LO:(q + 1) * LO]
    if cut(3):
        return

    table = tab[...].astype(BF16)
    count = iota((LO, NS), 0).astype(F32).astype(BF16)
    holds = lax.shift_right_logical(iota((TR, NS), 0), 2)
    low_half = iota((8, NS), 0) < NG
    one = jnp.ones((), BF16)
    zero = jnp.zeros((), BF16)

    def look(i, carry):
        got = []
        for u in range(4):
            idx = perm[pl.ds(i * 4 + u, 1), :]
            ilo = lax.bitwise_and(idx, LO - 1).astype(F32).astype(BF16)
            found = mm(table, jnp.where(count == ilo, one, zero))
            found = jnp.where(holds == lax.shift_right_logical(idx, 8), found, 0.0)
            part = found[0:8]
            for j in range(1, TR // 8):
                part = part + found[j * 8:(j + 1) * 8]
            got.append(part + pltpu.roll(part, NG, axis=0))
        rows = jnp.concatenate(
            [jnp.where(low_half, got[0], got[1]), jnp.where(low_half, got[2], got[3])], axis=0
        )
        yo[c, pl.ds(pl.multiple_of(i * 16, 16), 16), :] = rows.astype(BF16)
        return carry

    def sum_variants():
        for k in range(1, NZ):
            landed(("gr", k))
        gr[z] = gcp[z]
        tot = gr[0]
        for j in range(1, NZ):
            tot = tot + gr[j]
        mu = tot[GONE:GONE + 1, :] * (1.0 / NSAMP)
        between = jnp.zeros((1, 128), F32)
        for j in range(NZ):
            off = gr[j, GONE:GONE + 1, :] * (1.0 / (2 * NS)) - mu
            between = between + off * off
        centred = jnp.where(row < NC, tot - colmean * tot[GONE:GONE + 1, :], 0.0)
        slope = mm(gm[:, 0:GR], centred, HIGH)
        explained = jnp.sum(centred * slope, axis=0, keepdims=True)
        spread_all = tot[GSP:GSP + 1, :] + between * (2.0 * NS)
        weight = 1.0 / (jnp.maximum(spread_all - explained, 0.0) + EPS)
        ga[z] = jnp.where(row == GSP, weight, jnp.where(row == GONE, slope + mu, slope))
        for k in near:
            start(("ga", k), ga.at[z], ga.at[z], ga_s.at[k], ga_r.at[NZ - k], dev(zc(k), c, b),
                  ga.at[zc(k)], ga_r.at[k])

    for j in range(3):
        lax.fori_loop(j * 4, j * 4 + 4, look, 0)
        part = pl.ds(j * 64, 64)
        start(("yo", j), yo.at[c, part], yo.at[c, part], y_s.at[j], y_r.at[j], other,
              yo.at[oc, part], y_r.at[j])
        if j == 0:
            send_halo(1)
            sum_variants()
    if cut(4):
        return
    for j in range(3):
        landed(("yo", j))

    def product(kind, at):
        lanes = pl.ds(pl.multiple_of(at, 128), WIDTHS[kind])
        ds[kind][...] = mm(yo[0], gs[0, :, lanes]) + mm(yo[1], gs[1, :, lanes])

    def chunk(kind, k):
        return ds[kind].at[pl.ds(pl.multiple_of(zc(k) * CH, CH), CH)]

    def hops(kind, way):
        return HOPS[(kind + way) % 2]

    def unpack(ref, scale):
        q = ref[...].astype(F32)
        return [q[CH * h:CH * (h + 1)] * scale[h:h + 1, :] for h in range(2)]

    def halves(ref):
        w = ref.shape[1] // 2
        return [ref[:, w * h:w * (h + 1)] for h in range(2)]

    def pack(parts, ref, scale):
        codes = []
        for h in range(2):
            top = jnp.max(jnp.abs(parts[h]), axis=0, keepdims=True)
            top = jnp.maximum(top, TINY)
            scale[h:h + 1, :] = top * (1.0 / QMAX)
            codes.append(jnp.round(parts[h] * (QMAX / top)))
        ref[...] = jnp.concatenate(codes, axis=0).astype(jnp.int32).astype(jnp.int16)

    def send_sum(kind, way, t):
        n = hops(kind, way)
        sign = 1 - 2 * way
        parts = halves(chunk(kind, -sign * (n - t)))
        if t == 0:
            src, scale = q0[kind].at[way], s0[kind].at[way]
        else:
            src, scale = rb[kind].at[way, t - 1], sb[kind].at[way, t - 1]
            landed(("rs", kind, way, t - 1))
            landed(("sc", kind, way, t - 1))
            parts = [u + v for u, v in zip(parts, unpack(src, scale))]
        pack(parts, src, scale)
        to = dev(zc(-sign), c, b)
        for i, (name, here, buf) in enumerate((("rs", src, rb), ("sc", scale, sb))):
            land = buf[kind].at[way, t]
            start((name, kind, way, t), here, land, rs_s.at[i, kind, way, t],
                  rs_r.at[i, kind, way, t], to, land, rs_r.at[i, kind, way, t])

    product(0, own_at)
    send_sum(0, 0, 0)
    send_sum(0, 1, 0)

    proj = jnp.concatenate(
        [nt(yo[0], xp[0]) + nt(yo[1], xp[1]), jnp.zeros((ROWS, 128 - XR), F32)], axis=1
    )
    proj = jnp.where(iota((ROWS, 128), 1) < GONE, proj, pltpu.roll(proj, 128 - (ONE - GONE), axis=1))
    lane8 = iota((8, 128), 1)
    for j in range(NZ):
        p3 = [proj[CH * j + 8 * i:CH * j + 8 * i + 8] for i in range(3)]
        pq[j] = jnp.where(
            lane8 < GR, p3[0],
            jnp.where(lane8 < 2 * GR, pltpu.roll(p3[1], GR, axis=1),
                      pltpu.roll(p3[2], 2 * GR, axis=1)),
        )
    for k in near:
        start(("pr", k), pq.at[zc(k)], pr.at[z], pr_s.at[k], pr_r.at[NZ - k], dev(zc(k), c, b),
              pr.at[zc(k)], pr_r.at[k])
    landed(("h", 0, 0))
    landed(("h", 0, 1))
    product(1, halo_at)
    send_sum(1, 1, 0)
    send_sum(1, 0, 0)
    if cut(5):
        return

    order = ((0, 0), (0, 1), (1, 1), (1, 0))
    for kind, way in order:
        send_sum(kind, way, 1)

    landed(("h", 1, 0))
    landed(("h", 1, 1))
    product(2, halo_at + WA)
    for k in near:
        pack(halves(chunk(2, k)), qd.at[zc(k)], sd.at[zc(k)])
        for i, (name, here, there) in enumerate((("dr", qd, rd), ("dc", sd, td))):
            start((name, k), here.at[zc(k)], there.at[z], d_s.at[i, k], d_r.at[i, NZ - k],
                  dev(zc(k), c, b), there.at[zc(k)], d_r.at[i, k])
    for k in range(1, NZ):
        landed(("ga", k))
    start("gh", ga, gh, gh_s, gh_r, dev(z, oc, nbr), gh, gh_r)

    for kind, way in order:
        send_sum(kind, way, 2)

    gene24 = lax.rem(iota((CH, 1), 0), NG)
    first = jnp.zeros((CH, 1), jnp.int32)
    last = jnp.zeros((CH, 1), jnp.int32)
    for g in range(NG):
        first = jnp.where(gene24 == g, win[0, b * NG + g], first)
        last = jnp.where(gene24 == g, win[1, b * NG + g], last)
    base = b * VB - VH + c * VB + iota((CH, VH), 1)

    for k in range(1, NZ):
        landed(("pr", k))
    pr[z] = pq[z]
    tot = pr[0]
    for j in range(1, NZ):
        tot = tot + pr[j]
    proj = jnp.concatenate(
        [tot, pltpu.roll(tot, 128 - GR, axis=1), pltpu.roll(tot, 128 - 2 * GR, axis=1)], axis=0
    )
    l24 = iota((CH, 128), 1)
    proj = jnp.where((l24 < NC) | (l24 == GONE), proj, 0.0)[:, 0:GR]

    for kind, way in order:
        if hops(kind, way) > 3:
            send_sum(kind, way, 3)

    def fit(ref, kinds):
        both = jnp.concatenate([ref[j] for j in range(NZ)], axis=1)
        lines = pl.ds(pl.multiple_of(z * CH, CH), CH)
        for kind, at, skip in kinds:
            beta_g = both[:, skip:skip + WIDTHS[kind]]
            ds[kind][lines, :] = ds[kind][lines, :] - mm(proj, beta_g, HIGH)
            pos = base[:, 0:WIDTHS[kind]] + at
            inside = (pos >= first) & (pos < last)
            wm[kind][...] = jnp.where(inside, beta_g[GSP:GSP + 1, :], 0.0)

    fit(ga, ((0, own_at, 0),))
    landed("gh")
    fit(gh, ((1, halo_at, 0), (2, halo_at + WA, WA)))

    def squares(kind, parts):
        v = jnp.concatenate(parts, axis=1)
        v = v * v * wm[kind][...]
        return functools.reduce(
            jnp.maximum, [v[:, i:i + 128] for i in range(0, WIDTHS[kind], 128)]
        )

    parts = halves(chunk(2, 0))
    for k in near:
        landed(("dr", k))
        landed(("dc", k))
        parts = [u + v for u, v in zip(parts, unpack(rd.at[zc(k)], td.at[zc(k)]))]
    best = squares(2, parts)
    for kind in range(2):
        parts = halves(chunk(kind, 0))
        for way in (0, 1) if hops(kind, 1) > 3 else (1, 0):
            end = hops(kind, way) - 1
            landed(("rs", kind, way, end))
            landed(("sc", kind, way, end))
            got = unpack(rb[kind].at[way, end], sb[kind].at[way, end])
            parts = [u + v for u, v in zip(parts, got)]
        best = jnp.maximum(best, squares(kind, parts))
    if cut(6):
        return
    best = jnp.max(best, axis=1, keepdims=True) * float(NSAMP)

    r24, l24 = iota((CH, 128), 0), iota((CH, 128), 1)
    placed = jnp.where(l24 == lax.shift_right_logical(r24, 2) + PZ * z, best, 0.0)
    placed = (placed[0:8] + placed[8:16]) + placed[16:24]
    fm[c, z] = (placed + pltpu.roll(placed, NG, axis=0))[0:NG]
    for cc in range(2):
        to = lax.rem(c + cc, 2)
        for k in near + ((0,) if cc else ()):
            start(("o", cc, k), fm.at[c, z], fm.at[c, z], o_s.at[cc, k],
                  o_r.at[cc, (NZ - k) % NZ], dev(zc(k), to, b), fm.at[to, zc(k)], o_r.at[cc, k])
    for key in [("o", 1, 0)] + [("o", cc, k) for k in near for cc in range(2)]:
        landed(key)
    both = [fm[cc, 0] for cc in range(2)]
    for j in range(1, NZ):
        both = [v + fm[cc, j] for cc, v in enumerate(both)]
    peak = jnp.maximum(both[0], both[1])
    columns = jnp.concatenate([peak, peak], axis=0).T
    level = LEVMAX * iota((NP, 128), 1).astype(F32) / (LEVELS - 1)
    out_ref[0:NG, :] = peak
    for g in range(NG):
        curve = jax.nn.sigmoid(columns[0:NP, g:g + 1] - level)
        out_ref[NG + g:NG + g + 1, :] = jnp.sum(curve, axis=0, keepdims=True) * (1.0 / NP)
    stop()


def split(both_ref, cur_ref, peak_ref):
    peak_ref[...] = both_ref[0:NG, 0:NP]
    cur_ref[...] = both_ref[NG:2 * NG, 0:LEVELS]


def per_device(upto, geno, covar, pheno, perm, windows):
    dma = pltpu.SemaphoreType.DMA
    vmem = pltpu.VMEM
    spec = pl.BlockSpec(memory_space=pltpu.VMEM)
    both = pl.pallas_call(
        functools.partial(kernel, upto),
        out_shape=jax.ShapeDtypeStruct((2 * NG, 128), F32),
        in_specs=[pl.BlockSpec(memory_space=pltpu.HBM)] * 5,
        out_specs=spec,
        scratch_shapes=[
            vmem((NP, NS), jnp.int32),
            pltpu.SMEM((2, NG * NB), jnp.int32),
            vmem((NZ, NC, NS), BF16),
            vmem((NZ, NG, NS), F32),
            vmem((2, XR, NS), BF16),
            vmem((2, NS, VB), BF16),
            vmem((2, GR, 128), F32),
            vmem((NZ, 16, 128), F32),
            vmem((GR, 128), F32),
            vmem((NZ, GR, 128), F32),
            vmem((NZ, GR, 128), F32),
            vmem((NZ, GR, 128), F32),
            vmem((NZ, GR, 128), F32),
            vmem((2, NZ, NG, NS), F32),
            vmem((TR, LO), F32),
            vmem((2, ROWS, NS), BF16),
            [vmem((ROWS, w), F32) for w in WIDTHS],
            vmem((NZ, 8, 128), F32),
            vmem((NZ, 8, 128), F32),
            [vmem((2, 2 * CH, w // 2), I16) for w in WIDTHS[:2]],
            [vmem((2, 2, w // 2), F32) for w in WIDTHS[:2]],
            [vmem((2, 4, 2 * CH, w // 2), I16) for w in WIDTHS[:2]],
            [vmem((2, 4, 2, w // 2), F32) for w in WIDTHS[:2]],
            vmem((NZ, 2 * CH, WB // 2), I16),
            vmem((NZ, 2, WB // 2), F32),
            vmem((NZ, 2 * CH, WB // 2), I16),
            vmem((NZ, 2, WB // 2), F32),
            [vmem((CH, w), F32) for w in WIDTHS],
            vmem((2, NZ, NG, 128), F32),
            dma((4,)), dma,
            dma, dma, dma, dma,
            dma((NZ,)), dma((NZ,)),
            dma((2, NZ)), dma((2, NZ)),
            dma, dma,
            dma((2, 2)), dma((2, 2)),
            dma((NZ,)), dma((NZ,)),
            dma((NZ,)), dma((NZ,)),
            dma, dma, dma, dma,
            dma((3,)), dma((3,)),
            dma((NZ,)), dma((NZ,)),
            dma((2, 2, 2, 4)), dma((2, 2, 2, 4)),
            dma((2, NZ)), dma((2, NZ)),
            dma((2, NZ)), dma((2, NZ)),
        ],
        compiler_params=pltpu.CompilerParams(
            collective_id=0, has_side_effects=True, vmem_limit_bytes=56 * 1024 * 1024
        ),
        name="scan",
    )(geno, covar.T, pheno.T, perm, windows.T)
    return pl.pallas_call(
        split,
        out_shape=(
            jax.ShapeDtypeStruct((NG, LEVELS), F32),
            jax.ShapeDtypeStruct((NG, NP), F32),
        ),
        in_specs=[spec],
        out_specs=(spec, spec),
        name="split",
    )(both)


def build(mesh, upto):
    in_specs = (P("samp", "var"), P("samp", None), P("samp", "var"), P(None, "samp"), P())
    out_specs = (P("var", None), P("var", None))
    return jax.shard_map(
        functools.partial(per_device, upto), mesh=mesh, in_specs=in_specs, out_specs=out_specs,
        check_vma=False,
    )


def solution(mesh):
    return build(mesh, 9)
```
